512 devices in a mesh: blk: 128 (over x, z, y_hi), grp: 4 (over y_lo, core).
Axes of the slice: x: 4, y: 4 (y_hi: 2, y_lo: 2; y = y_hi * 2 + y_lo), z: 16, core: 2. Of those that a mesh axis runs over, the one named last changes fastest.
Arguments:
- molecules: bfloat16 [16384, 640], P(('blk', 'grp')), may hold values from -2 to 2
- texts: bfloat16 [16384, 640], P(('blk', 'grp')), may hold values from -2 to 2
Outputs:
- molecule_grad: float32 [16384, 640], P(('blk', 'grp'))
- text_grad: float32 [16384, 640], P(('blk', 'grp'))
The draws below stay inside these ranges and needn't reach their ends.
All inputs are finite; a program needn't handle non-finite values.
Results may differ from the reference program's by a relative error of at most 0.0055.
Values may be sent and summed in bfloat16 or wider, within the bound.
A program may use at most 64 MiB of HBM per device.

```python
import math
import jax
import jax.numpy as jnp
from jax import lax

D = 640
ROWS = 32
PAIRS = 16384
N_GRP = 4


def pair_draw(key, boosted, boost_scale):
    key_basis, key_scale, key_order = jax.random.split(key, 3)
    partner_order = jax.random.permutation(key_order, PAIRS)
    basis = jnp.clip(jax.random.normal(key_basis, (PAIRS, D), jnp.float32), -5.0, 5.0) / math.sqrt(D)
    scales = jnp.exp(jax.random.uniform(key_scale, (PAIRS, 1), jnp.float32, math.log(0.4), math.log(3.5)))
    scales = jnp.where((partner_order < boosted)[:, None], boost_scale, scales)
    return (basis * scales, partner_order, scales)


def draw_molecules(key, part):
    boosted = 0
    boost_scale = 1.0
    values, partner_order, scales = pair_draw(key, boosted, boost_scale)
    return jnp.clip(values, -2.0, 2.0).astype(jnp.bfloat16)


def draw_texts(key, part):
    boosted = 0
    boost_scale = 1.0
    values, partner_order, scales = pair_draw(key, boosted, boost_scale)
    key = jax.random.fold_in(key, 7)
    jitter = jnp.clip(jax.random.normal(key, (PAIRS, D), jnp.float32), -5.0, 5.0) / math.sqrt(D) * scales
    partner = values[partner_order]
    mixed = 0.6 * values + 0.6 * partner + 0.45 * jitter
    return jnp.clip(mixed, -2.0, 2.0).astype(jnp.bfloat16)


def setup_inputs(seed: int = 0) -> dict:
    key_of = jax.random.split(jax.random.key(seed), 3)
    return {
        "molecules": draw_molecules(jax.random.fold_in(key_of[2], 71), 0),
        "texts": draw_texts(jax.random.fold_in(key_of[2], 71), 0),
    }


INVERSE_TEMP = 1.0 / 0.07
NEG_FILL = -1e30


def reference(molecules, texts):
    total_pairs = molecules.shape[0]
    features = molecules.shape[1]
    height = ROWS * N_GRP
    block_count = total_pairs // height
    mol_blocks = molecules.reshape(block_count, height, features)

    def first_pass(carried, mol_block):
        column_top, column_mass = carried
        scores = jnp.dot(mol_block, texts.T, preferred_element_type=jnp.float32) * INVERSE_TEMP
        raised = jnp.maximum(column_top, jnp.max(scores, axis=0))
        column_mass = column_mass * jnp.exp(column_top - raised) + jnp.sum(jnp.exp(scores - raised[None, :]), axis=0)
        row_top = jnp.max(scores, axis=1)
        row_lse = row_top + jnp.log(jnp.sum(jnp.exp(scores - row_top[:, None]), axis=1))
        return (raised, column_mass), row_lse

    initial = (jnp.full((total_pairs,), NEG_FILL, jnp.float32), jnp.zeros((total_pairs,), jnp.float32))
    (column_top, column_mass), row_lse = lax.scan(first_pass, initial, mol_blocks)
    col_lse = column_top + jnp.log(column_mass)
    starts = (jnp.arange(block_count, dtype=jnp.int32) * height).astype(jnp.int32)
    column_ids = jnp.arange(total_pairs, dtype=jnp.int32)

    def second_pass(summed, element):
        mol_block, row_part, first_row = element
        scores = jnp.dot(mol_block, texts.T, preferred_element_type=jnp.float32) * INVERSE_TEMP
        row_ids = first_row + jnp.arange(height, dtype=jnp.int32)
        paired = (row_ids[:, None] == column_ids[None, :]).astype(jnp.float32)
        weights = (0.5 * jnp.exp(scores - row_part[:, None]) + 0.5 * jnp.exp(scores - col_lse[None, :]) - paired).astype(jnp.bfloat16)
        mol_part = jnp.dot(weights, texts, preferred_element_type=jnp.float32) * INVERSE_TEMP
        summed = summed + jnp.dot(weights.T, mol_block, preferred_element_type=jnp.float32) * INVERSE_TEMP
        return summed, mol_part

    text_grad, mol_parts = lax.scan(second_pass, jnp.zeros((total_pairs, features), jnp.float32), (mol_blocks, row_lse, starts))
    return mol_parts.reshape(total_pairs, features), text_grad
```

```python
import jax
import jax.numpy as jnp
from jax import lax
from jax.experimental import pallas as pl
from jax.experimental.pallas import tpu as pltpu
from jax.sharding import PartitionSpec as P

INVERSE_TEMP = 1.0 / 0.07
LOG2E = 1.4426950408889634
MESH = pl.DeviceIdType.MESH
F32 = jnp.float32
BF16 = jnp.bfloat16
D = 640
SHARD = 32
HALF = 16
MOLS = 1024
TEXTS = 512


def place():
    blk, grp = lax.axis_index("blk"), lax.axis_index("grp")
    x = lax.div(blk, 32)
    z = lax.rem(lax.div(blk, 2), 16)
    y = lax.rem(blk, 2) * 2 + lax.div(grp, 2)
    return x, y, lax.div(z, 2), lax.rem(z, 2), lax.rem(grp, 2)


def device(x, y, p, q, c):
    return ((x * 16 + p * 2 + q) * 2 + lax.div(y, 2), lax.rem(y, 2) * 2 + c)


def kernel(
    mol_in, text_in, out,
    mol, text, scores, weights, row_wide, col_top, col_mass, row_part, col_part,
    mol_sum, mol_send, mol_recv1, mol_send2, mol_recv2, mol_send3, mol_recv3,
    text_sum, text_send, text_recv0, text_send1, text_recv1, text_recv2,
    load_sem, pair_sem, mol1_sem, mol2_sem, near_sem, far_sem, sib_sem,
    row_sem, col_sem, rs_sib_sem, rs_text_sem, rs_mol1_sem, rs_mol2_sem, rs_pair_sem,
):
    x, y, p, q, c = place()

    def plus(v, d, n):
        return lax.rem(v + (d + n) % n, n)

    def x_peer(d):
        return device(plus(x, d, 4), y, p, q, c)

    def y_peer(d):
        return device(x, plus(y, d, 4), p, q, c)

    def p_peer(d):
        return device(x, y, plus(p, d, 8), q, c)

    partner = device(x, y, p, 1 - q, c)
    sibling = device(x, y, p, q, 1 - c)

    def send(src, dst, sems, index, target):
        copy = pltpu.make_async_remote_copy(
            src_ref=src,
            dst_ref=dst,
            send_sem=sems.at[(0,) + index],
            recv_sem=sems.at[(1,) + index],
            device_id=target,
            device_id_type=MESH,
        )
        copy.start()
        return copy

    started = []

    def rows(start, size):
        return pl.ds(pl.multiple_of(start, 16), size)

    def mol_row(h, x_, y_):
        return (y_ * 4 + x_) * SHARD if h == 0 else MOLS // 2 + (x_ * 4 + y_) * SHARD

    def text_row(p_, c_):
        return (c_ * 8 + p_) * SHARD

    own_row = [mol_row(0, x, y) + q * HALF, mol_row(1, x, y) + q * HALF]
    partner_row = [mol_row(0, x, y) + (1 - q) * HALF, mol_row(1, x, y) + (1 - q) * HALF]
    loads = [
        pltpu.make_async_copy(mol_in.at[pl.ds(0, HALF)], mol.at[rows(own_row[0], HALF)], load_sem.at[0]),
        pltpu.make_async_copy(mol_in.at[pl.ds(HALF, HALF)], mol.at[rows(own_row[1], HALF)], load_sem.at[1]),
        pltpu.make_async_copy(text_in, text.at[rows(text_row(p, c), SHARD)], load_sem.at[2]),
    ]
    for load in loads:
        load.start()

    peers = [p_peer(d) for d in (1, -1, 2, -2)] + [partner, sibling]
    peers += [x_peer(d) for d in (1, 2, 3)] + [y_peer(d) for d in (1, 2, 3)]
    barrier = pltpu.get_barrier_semaphore()
    for peer in peers:
        pl.semaphore_signal(barrier, inc=1, device_id=peer, device_id_type=MESH)
    pl.semaphore_wait(barrier, len(peers))
    for load in loads:
        load.wait()

    def text_send_rows(p_, c_, sems, index, target, first=0, size=SHARD):
        block = text.at[rows(text_row(p_, c_) + first, size)]
        copy = send(block, block, sems, index, target)
        started.append(copy)
        return copy

    def mol_send_rows(start, size, sems, index, target):
        block = mol.at[rows(start, size)]
        copy = send(block, block, sems, index, target)
        started.append(copy)
        return copy

    first_peer = [x_peer, y_peer]
    second_peer = [y_peer, x_peer]
    two = {d: text_send_rows(p, c, near_sem, (i,), p_peer(d)) for i, d in ((0, 2), (1, -2))}
    pair = [mol_send_rows(own_row[h], HALF, pair_sem, (h,), partner) for h in (0, 1)]
    stage1 = {}
    for d in (1, 3, 2):
        for h in (0, 1):
            stage1[h, 0, d] = mol_send_rows(own_row[h], HALF, mol1_sem, (h, 0, d), first_peer[h](d))
    one = {d: text_send_rows(p, c, near_sem, (i,), p_peer(d)) for i, d in ((2, 1), (3, -1))}
    sib = [text_send_rows(p, c, sib_sem, (0,), sibling)]
    for h in (0, 1):
        pair[h].wait_recv()
    for d in (1, 3, 2):
        for h in (0, 1):
            stage1[h, 1, d] = mol_send_rows(partner_row[h], HALF, mol1_sem, (h, 1, d), first_peer[h](d))
    stage2 = []

    def spread(e):
        xe, ye = plus(x, e, 4), plus(y, e, 4)
        starts = [mol_row(0, xe, y), mol_row(1, x, ye)]
        for d in (1, 3, 2):
            for h in (0, 1):
                stage2.append(mol_send_rows(starts[h], SHARD, mol2_sem, (h, e, d), second_peer[h](d)))

    spread(0)
    for e in (1, 3):
        for h in (0, 1):
            stage1[h, 0, (4 - e) % 4].wait_recv()
            stage1[h, 1, (4 - e) % 4].wait_recv()
        spread(e)
    far = []
    for i, d in ((0, 2), (1, -2)):
        two[d].wait_recv()
        back = plus(p, -d, 8)
        far.append(text_send_rows(back, c, far_sem, (2 + i,), p_peer(d), i * HALF, HALF))
        far.append(text_send_rows(back, c, far_sem, (i,), p_peer(d // 2)))
        sib.append(text_send_rows(back, c, sib_sem, (1 + i,), sibling))
    for h in (0, 1):
        stage1[h, 0, 2].wait_recv()
        stage1[h, 1, 2].wait_recv()
    spread(2)
    for i, d in ((3, 1), (4, -1)):
        one[d].wait_recv()
        sib.append(text_send_rows(plus(p, -d, 8), c, sib_sem, (i,), sibling))
    for copy in far:
        copy.wait_recv()
    sib.append(text_send_rows(plus(p, 3, 8), c, sib_sem, (5,), sibling))
    sib.append(text_send_rows(plus(p, -3, 8), c, sib_sem, (6,), sibling))
    sib.append(text_send_rows(plus(p, 4, 8), c, sib_sem, (7,), sibling))
    for copy in stage2:
        copy.wait_recv()
    for copy in sib:
        copy.wait_recv()

    scores[...] = lax.dot_general(
        mol[...], text[...], (((1,), (1,)), ((), ())), preferred_element_type=F32
    ) * (INVERSE_TEMP * LOG2E)
    row_me = (x * 4 + y) * 2 + q
    col_me = c * 8 + p
    lanes = [slice(128 * k, 128 * k + 128) for k in range(TEXTS // 128)]

    def totals(b, carry):
        block = pl.ds(pl.multiple_of(b * 128, 128), 128)
        parts = [scores[block, lane] for lane in lanes]
        top = jnp.maximum(jnp.maximum(parts[0], parts[1]), jnp.maximum(parts[2], parts[3]))
        mass = sum(jnp.exp2(part - top) for part in parts)
        top, mass = top.T, mass.T
        overall = jnp.max(top, axis=0, keepdims=True)
        mass = jnp.sum(mass * jnp.exp2(top - overall), axis=0, keepdims=True)
        row_part[row_me, pl.ds(b, 1), :] = overall + jnp.log2(mass)
        for part, lane in zip(parts, lanes):
            tiles = part.reshape(16, 8, 128)
            top = jnp.max(tiles, axis=0)
            col_top[b, :, lane] = top
            col_mass[b, :, lane] = jnp.sum(jnp.exp2(tiles - top[None]), axis=0)
        return carry

    lax.fori_loop(0, MOLS // 128, totals, 0)
    for k, lane in enumerate(lanes):
        top = col_top[:, :, lane].reshape(64, 128)
        overall = jnp.max(top, axis=0, keepdims=True)
        mass = jnp.sum(col_mass[:, :, lane].reshape(64, 128) * jnp.exp2(top - overall), axis=0, keepdims=True)
        col_part[col_me, pl.ds(k, 1), :] = overall + jnp.log2(mass)

    exchange = []
    for d in (4, 3, 5, 2, 6, 1, 7, 0):
        for e in (0, 1):
            if d or e:
                block = col_part.at[col_me, pl.ds(0, 4)]
                target = device(x, y, plus(p, d, 8), q, c if e == 0 else 1 - c)
                exchange.append(send(block, block, col_sem, (d * 2 + e,), target))
    for dx in (2, 1, 3, 0):
        for dy in (2, 1, 3, 0):
            for e in (0, 1):
                if dx or dy or e:
                    block = row_part.at[row_me]
                    target = device(plus(x, dx, 4), plus(y, dy, 4), p, q if e == 0 else 1 - q, c)
                    exchange.append(send(block, block, row_sem, ((dx * 4 + dy) * 2 + e,), target))
    for copy in exchange:
        copy.wait_recv()
    started.extend(exchange)

    def merge(parts):
        top = jnp.max(parts, axis=0)
        return top + jnp.log2(jnp.sum(jnp.exp2(parts - top[None]), axis=0))

    row_lse = merge(row_part[...])
    col_lse = merge(col_part[:, 0:4, :])

    for b in range(MOLS // 128):
        row_wide[128 * b : 128 * b + 128, :] = jnp.broadcast_to(row_lse[b : b + 1, :], (128, 128)).T

    def weigh(part, row, k):
        return 0.5 * jnp.exp2(part - row) + 0.5 * jnp.exp2(part - col_lse[k : k + 1, :])

    def weight(b, carry):
        block = pl.ds(pl.multiple_of(b * 128, 128), 128)
        row = row_wide[block, :]
        for k, lane in enumerate(lanes):
            weights[block, lane] = weigh(scores[block, lane], row, k).astype(BF16)
        return carry

    lax.fori_loop(0, MOLS // 128, weight, 0)
    for h in (0, 1):
        block = rows(own_row[h], HALF)
        row = row_wide[block, :]
        ahead = lax.broadcasted_iota(jnp.int32, (HALF, 128), 1) - lax.broadcasted_iota(jnp.int32, (HALF, 128), 0)
        for k, lane in enumerate(lanes):
            paired = (ahead == text_row(p, c) + h * HALF - 128 * k).astype(F32)
            weights[block, lane] = (weigh(scores[block, lane], row, k) - paired).astype(BF16)

    text_sum[...] = lax.dot_general(
        weights[...], mol[...], (((0,), (0,)), ((), ())), preferred_element_type=F32
    )
    other = rows((1 - c) * (TEXTS // 2), TEXTS // 2)
    text_send[...] = text_sum[other, :].astype(BF16)
    rs_sib = send(text_send, text_recv0, rs_sib_sem, (0,), sibling)
    started.append(rs_sib)

    mol_sum[...] = jnp.dot(weights[...], text[...], preferred_element_type=F32)
    mol_send[...] = mol_sum[...].astype(BF16)
    quarter = 4 * SHARD
    rs_mol1 = {}
    for d in (2, 1, 3):
        for h in (0, 1):
            there = (plus(y, d, 4) if h == 0 else plus(x, d, 4)) * quarter + h * (MOLS // 2)
            rs_mol1[h, d] = send(
                mol_send.at[rows(there, quarter)], mol_recv1.at[h, d], rs_mol1_sem, (h, d), second_peer[h](d)
            )
            started.append(rs_mol1[h, d])

    rs_sib.wait_recv()
    mine = rows(c * (TEXTS // 2), TEXTS // 2)
    text_sum[mine, :] = text_sum[mine, :] + text_recv0[...].astype(F32)
    rs_text = {}

    def text_block(d):
        return text_sum[rows(text_row(plus(p, d, 8), c), SHARD), :]

    for i, d in enumerate((3, -3, 4, 1, -1)):
        text_send1[i] = text_block(d).astype(BF16)
    rs_text["4a"] = send(
        text_send1.at[2, pl.ds(0, HALF)], text_recv1.at[2, pl.ds(0, HALF)], rs_text_sem, (2,), p_peer(2)
    )
    rs_text["4b"] = send(
        text_send1.at[2, pl.ds(HALF, HALF)], text_recv1.at[2, pl.ds(HALF, HALF)], rs_text_sem, (3,), p_peer(-2)
    )
    rs_text[3] = send(text_send1.at[0], text_recv1.at[0], rs_text_sem, (0,), p_peer(1))
    rs_text[-3] = send(text_send1.at[1], text_recv1.at[1], rs_text_sem, (1,), p_peer(-1))
    rs_text[1] = send(text_send1.at[3], text_recv2.at[0], rs_text_sem, (4,), p_peer(1))
    rs_text[-1] = send(text_send1.at[4], text_recv2.at[1], rs_text_sem, (5,), p_peer(-1))

    rs_mol2 = {}
    for h in (0, 1):
        base = (y if h == 0 else x) * quarter + h * (MOLS // 2)
        for d in (1, 3, 2):
            rs_mol1[h, d].wait_recv()
        block = mol_sum[rows(base, quarter), :]
        for d in (1, 2, 3):
            block = block + mol_recv1[h, d].astype(F32)
        mol_sum[rows(base, quarter), :] = block
        for d in (2, 1, 3):
            there = base + (plus(x, d, 4) if h == 0 else plus(y, d, 4)) * SHARD
            mol_send2[h, d] = mol_sum[rows(there, SHARD), :].astype(BF16)
            rs_mol2[h, d] = send(mol_send2.at[h, d], mol_recv2.at[h, d], rs_mol2_sem, (h, d), first_peer[h](d))

    for name in ("4a", "4b", 3, -3):
        rs_text[name].wait_recv()
    ahead = text_block(2) + text_recv1[0].astype(F32)
    text_send1[5, pl.ds(0, HALF)] = (ahead[:HALF] + text_recv1[2, pl.ds(0, HALF)].astype(F32)).astype(BF16)
    text_send1[5, pl.ds(HALF, HALF)] = ahead[HALF:].astype(BF16)
    rs_text[2] = send(text_send1.at[5], text_recv2.at[2], rs_text_sem, (6,), p_peer(2))
    behind = text_block(-2) + text_recv1[1].astype(F32)
    text_send1[6, pl.ds(0, HALF)] = behind[:HALF].astype(BF16)
    text_send1[6, pl.ds(HALF, HALF)] = (behind[HALF:] + text_recv1[2, pl.ds(HALF, HALF)].astype(F32)).astype(BF16)
    rs_text[-2] = send(text_send1.at[6], text_recv2.at[3], rs_text_sem, (7,), p_peer(-2))

    rs_pair = []
    for h in (0, 1):
        for d in (1, 3, 2):
            rs_mol2[h, d].wait_recv()
        here = mol_row(h, x, y)
        block = mol_sum[rows(here, SHARD), :]
        for d in (1, 2, 3):
            block = block + mol_recv2[h, d].astype(F32)
        mol_sum[rows(here, SHARD), :] = block
        mol_send3[h] = mol_sum[rows(partner_row[h], HALF), :].astype(BF16)
        rs_pair.append(send(mol_send3.at[h], mol_recv3.at[h], rs_pair_sem, (h,), partner))
    for h in (0, 1):
        rs_pair[h].wait_recv()
        out[0, pl.ds(HALF * h, HALF), :] = (
            mol_sum[rows(own_row[h], HALF), :] + mol_recv3[h].astype(F32)
        ) * INVERSE_TEMP
    total = text_block(0)
    for i, d in enumerate((1, -1, 2, -2)):
        rs_text[d].wait_recv()
        total = total + text_recv2[i].astype(F32)
    out[1] = total * INVERSE_TEMP

    started.extend(rs_text.values())
    started.extend(rs_mol2.values())
    started.extend(rs_pair)
    for copy in started:
        copy.wait_send()


def on_device(molecules, texts):
    dma = pltpu.SemaphoreType.DMA
    both = pl.pallas_call(
        kernel,
        out_shape=jax.ShapeDtypeStruct((2, SHARD, D), F32),
        in_specs=[pl.BlockSpec(memory_space=pl.ANY)] * 2,
        out_specs=pl.BlockSpec(memory_space=pltpu.VMEM),
        scratch_shapes=[
            pltpu.VMEM((MOLS, D), BF16),
            pltpu.VMEM((TEXTS, D), BF16),
            pltpu.VMEM((MOLS, TEXTS), F32),
            pltpu.VMEM((MOLS, TEXTS), BF16),
            pltpu.VMEM((MOLS, 128), F32),
            pltpu.VMEM((8, 8, TEXTS), F32),
            pltpu.VMEM((8, 8, TEXTS), F32),
            pltpu.VMEM((32, 8, 128), F32),
            pltpu.VMEM((16, 8, 128), F32),
            pltpu.VMEM((MOLS, D), F32),
            pltpu.VMEM((MOLS, D), BF16),
            pltpu.VMEM((2, 4, 4 * SHARD, D), BF16),
            pltpu.VMEM((2, 4, SHARD, D), BF16),
            pltpu.VMEM((2, 4, SHARD, D), BF16),
            pltpu.VMEM((2, HALF, D), BF16),
            pltpu.VMEM((2, HALF, D), BF16),
            pltpu.VMEM((TEXTS, D), F32),
            pltpu.VMEM((TEXTS // 2, D), BF16),
            pltpu.VMEM((TEXTS // 2, D), BF16),
            pltpu.VMEM((7, SHARD, D), BF16),
            pltpu.VMEM((3, SHARD, D), BF16),
            pltpu.VMEM((4, SHARD, D), BF16),
            dma((3,)),
            dma((2, 2)),
            dma((2, 2, 2, 4)),
            dma((2, 2, 4, 4)),
            dma((2, 4)),
            dma((2, 4)),
            dma((2, 8)),
            dma((2, 32)),
            dma((2, 16)),
            dma((2, 1)),
            dma((2, 8)),
            dma((2, 2, 4)),
            dma((2, 2, 4)),
            dma((2, 2)),
        ],
        compiler_params=pltpu.CompilerParams(
            collective_id=0, has_side_effects=True, vmem_limit_bytes=40 << 20
        ),
    )(molecules, texts)
    return both[0], both[1]


def solution(mesh):
    spec = P(("blk", "grp"), None)
    return jax.shard_map(
        on_device, mesh=mesh, in_specs=(spec, spec), out_specs=(spec, spec), check_vma=False
    )
```

```python
import jax
import jax.numpy as jnp
from jax import lax
from jax.experimental import pallas as pl
from jax.experimental.pallas import tpu as pltpu
from jax.sharding import PartitionSpec as P

INVERSE_TEMP = 1.0 / 0.07
LOG2E = 1.4426950408889634
MESH = pl.DeviceIdType.MESH
F32 = jnp.float32
BF16 = jnp.bfloat16
D = 640
SHARD = 32
HALF = 16
MOLS = 1024
TEXTS = 512


def place():
    blk, grp = lax.axis_index("blk"), lax.axis_index("grp")
    x = lax.div(blk, 32)
    z = lax.rem(lax.div(blk, 2), 16)
    y = lax.rem(blk, 2) * 2 + lax.div(grp, 2)
    return x, y, lax.div(z, 2), lax.rem(z, 2), lax.rem(grp, 2)


def device(x, y, p, q, c):
    return ((x * 16 + p * 2 + q) * 2 + lax.div(y, 2), lax.rem(y, 2) * 2 + c)


def kernel(
    mol_in, text_in, out,
    mol, text, scores, by_row, weights, row_wide, col_top, col_mass, row_part, col_part,
    mol_sum, mol_send, mol_recv1, mol_send2, mol_recv2, mol_send3, mol_recv3,
    text_sum, text_send, text_recv0, text_send1, text_recv1,
    sent_sem, load_sem, pair_sem, mol1_sem, mol2_sem, near_sem, far_sem, sib_sem, row_sem, col_sem,
    rs_sib_sem, rs_text_sem, rs_mol1_sem, rs_mol2_sem, rs_pair_sem,
):
    x, y, p, q, c = place()

    def plus(v, d, n):
        return lax.rem(v + (d + n) % n, n)

    def x_peer(d):
        return device(plus(x, d, 4), y, p, q, c)

    def y_peer(d):
        return device(x, plus(y, d, 4), p, q, c)

    def p_peer(d):
        return device(x, y, plus(p, d, 8), q, c)

    partner = device(x, y, p, 1 - q, c)
    sibling = device(x, y, p, q, 1 - c)

    def send(src, dst, phase, sem, target):
        pltpu.make_async_remote_copy(
            src_ref=src,
            dst_ref=dst,
            send_sem=sent_sem.at[phase],
            recv_sem=sem,
            device_id=target,
            device_id_type=MESH,
        ).start()

    def await_bytes(ref, sem):
        pltpu.make_async_copy(ref, ref, sem).wait()

    def await_rows(count, sem):
        await_bytes(mol_sum.at[pl.ds(0, count // 2)], sem)

    def rows(start, size):
        return pl.ds(pl.multiple_of(start, 16), size)

    def mol_row(h, q_, x_, y_):
        return h * (MOLS // 2) + q_ * (MOLS // 4) + (y_ * 4 + x_ if h == 0 else x_ * 4 + y_) * HALF

    def text_row(p_, c_):
        return (c_ * 8 + p_) * SHARD

    other_q = 1 - q
    own_row = [mol_row(h, q, x, y) for h in (0, 1)]
    partner_row = [mol_row(h, other_q, x, y) for h in (0, 1)]
    loads = [
        pltpu.make_async_copy(mol_in.at[pl.ds(0, HALF)], mol.at[rows(own_row[0], HALF)], load_sem.at[0]),
        pltpu.make_async_copy(mol_in.at[pl.ds(HALF, HALF)], mol.at[rows(own_row[1], HALF)], load_sem.at[0]),
        pltpu.make_async_copy(text_in, text.at[rows(text_row(p, c), SHARD)], load_sem.at[0]),
    ]
    for load in loads:
        load.start()

    peers = [p_peer(d) for d in (1, -1, 2, -2)] + [partner, sibling]
    peers += [x_peer(d) for d in (1, 2, 3)] + [y_peer(d) for d in (1, 2, 3)]
    barrier = pltpu.get_barrier_semaphore()
    for peer in peers:
        pl.semaphore_signal(barrier, inc=1, device_id=peer, device_id_type=MESH)
    pl.semaphore_wait(barrier, len(peers))
    await_rows(2 * SHARD, load_sem.at[0])

    def text_send_rows(p_, c_, sem, target, first=0, size=SHARD):
        block = text.at[rows(text_row(p_, c_) + first, size)]
        send(block, block, 0, sem, target)

    def mol_send_rows(start, size, sem, target):
        block = mol.at[rows(start, size)]
        send(block, block, 0, sem, target)

    first_peer = [x_peer, y_peer]
    second_peer = [y_peer, x_peer]
    low, high = (0, HALF), (HALF, HALF)

    def fan(own):
        for d in (1, 3, 2):
            for h in (0, 1):
                start = own_row[h] if own else partner_row[h]
                mol_send_rows(start, HALF, mol1_sem.at[own, d], first_peer[h](d))

    def spread(own, e):
        q_ = q if own else other_q
        starts = [mol_row(0, q_, plus(x, e, 4), y), mol_row(1, q_, x, plus(y, e, 4))]
        for d in (1, 3, 2):
            for h in (0, 1):
                mol_send_rows(starts[h], HALF, mol2_sem.at[0], second_peer[h](d))

    def fan_arrived(own, e):
        await_rows(2 * HALF, mol1_sem.at[own, 4 - e])

    def to_sibling(d):
        text_send_rows(plus(p, d, 8), c, sib_sem.at[0], sibling)

    for h in (0, 1):
        mol_send_rows(own_row[h], HALF, pair_sem.at[0], partner)
    for i, (d, part) in enumerate(((2, low), (-2, high), (2, high), (-2, low))):
        text_send_rows(p, c, near_sem.at[i], p_peer(d), *part)
    fan(1)
    spread(1, 0)
    for d in (1, -1):
        text_send_rows(p, c, near_sem.at[4], p_peer(d))
    to_sibling(0)
    await_rows(2 * HALF, pair_sem.at[0])
    fan(0)
    spread(0, 0)
    for e in (1, 3, 2):
        fan_arrived(1, e)
        spread(1, e)

    def forward(i, source, d, part):
        text_send_rows(plus(p, source, 8), c, far_sem.at[i], p_peer(d), *part)

    await_rows(HALF, near_sem.at[0])
    forward(0, -2, 2, low)
    forward(1, -2, 1, low)
    await_rows(HALF, near_sem.at[1])
    forward(0, 2, -2, high)
    forward(1, 2, -1, high)
    for e in (1, 3, 2):
        fan_arrived(0, e)
        spread(0, e)
    await_rows(HALF, near_sem.at[2])
    forward(1, -2, 1, high)
    to_sibling(-2)
    await_rows(HALF, near_sem.at[3])
    forward(1, 2, -1, low)
    to_sibling(2)
    await_rows(2 * SHARD, near_sem.at[4])
    to_sibling(-1)
    to_sibling(1)
    await_rows(2 * SHARD, far_sem.at[1])
    to_sibling(-3)
    to_sibling(3)
    await_rows(SHARD, far_sem.at[0])
    to_sibling(4)
    await_rows(48 * HALF, mol2_sem.at[0])
    await_rows(8 * SHARD, sib_sem.at[0])
    await_rows(1472, sent_sem.at[0])

    scores[...] = lax.dot_general(
        mol[...], text[...], (((1,), (1,)), ((), ())), preferred_element_type=F32
    ) * (INVERSE_TEMP * LOG2E)
    row_me = (x * 4 + y) * 2 + q
    col_me = c * 8 + p
    lanes = [slice(128 * k, 128 * k + 128) for k in range(TEXTS // 128)]

    def column_totals(b, carry):
        for lane in lanes:
            tiles = scores[pl.ds(pl.multiple_of(b * 128, 128), 128), lane].reshape(16, 8, 128)
            top = jnp.max(tiles, axis=0)
            col_top[b, :, lane] = top
            col_mass[b, :, lane] = jnp.sum(jnp.exp2(tiles - top[None]), axis=0)
        return carry

    lax.fori_loop(0, MOLS // 128, column_totals, 0)
    for k, lane in enumerate(lanes):
        top = col_top[:, :, lane].reshape(64, 128)
        overall = jnp.max(top, axis=0, keepdims=True)
        mass = jnp.sum(col_mass[:, :, lane].reshape(64, 128) * jnp.exp2(top - overall), axis=0, keepdims=True)
        col_part[col_me, pl.ds(k, 1), :] = overall + jnp.log2(mass)
    for d in (4, 3, 5, 2, 6, 1, 7, 0):
        for e in (0, 1):
            if d or e:
                block = col_part.at[col_me, pl.ds(0, 4)]
                target = device(x, y, plus(p, d, 8), q, c if e == 0 else 1 - c)
                send(block, block, 1, col_sem.at[0], target)

    def row_totals(b, carry):
        block = pl.ds(pl.multiple_of(b * 128, 128), 128)
        parts = [scores[block, lane] for lane in lanes]
        top = jnp.maximum(jnp.maximum(parts[0], parts[1]), jnp.maximum(parts[2], parts[3]))
        mass = sum(jnp.exp2(part - top) for part in parts)
        top, mass = top.T, mass.T
        overall = jnp.max(top, axis=0, keepdims=True)
        mass = jnp.sum(mass * jnp.exp2(top - overall), axis=0, keepdims=True)
        row_part[row_me, pl.ds(b, 1), :] = overall + jnp.log2(mass)
        return carry

    lax.fori_loop(0, MOLS // 128, row_totals, 0)
    for dx in (2, 1, 3, 0):
        for dy in (2, 1, 3, 0):
            for e in (0, 1):
                if dx or dy or e:
                    block = row_part.at[row_me]
                    target = device(plus(x, dx, 4), plus(y, dy, 4), p, q if e == 0 else other_q, c)
                    send(block, block, 2, row_sem.at[0], target)

    def merge(parts):
        top = jnp.max(parts, axis=0)
        return top + jnp.log2(jnp.sum(jnp.exp2(parts - top[None]), axis=0))

    await_bytes(row_part.at[pl.ds(0, 31)], row_sem.at[0])
    row_lse = merge(row_part[...])
    for b in range(MOLS // 128):
        row_wide[128 * b : 128 * b + 128, :] = jnp.broadcast_to(row_lse[b : b + 1, :], (128, 128)).T

    def row_weight(b, carry):
        block = pl.ds(pl.multiple_of(b * 128, 128), 128)
        row = row_wide[block, :]
        for lane in lanes:
            by_row[block, lane] = 0.5 * jnp.exp2(scores[block, lane] - row)
        return carry

    lax.fori_loop(0, MOLS // 128, row_weight, 0)
    await_bytes(col_part.at[pl.ds(0, 15), pl.ds(0, 4)], col_sem.at[0])
    col_lse = merge(col_part[:, 0:4, :])

    def weigh(block, k):
        lane = lanes[k]
        return by_row[block, lane] + 0.5 * jnp.exp2(scores[block, lane] - col_lse[k : k + 1, :])

    def weight(b, carry):
        block = pl.ds(pl.multiple_of(b * 128, 128), 128)
        for k, lane in enumerate(lanes):
            weights[block, lane] = weigh(block, k).astype(BF16)
        return carry

    lax.fori_loop(0, MOLS // 128, weight, 0)
    for h in (0, 1):
        block = rows(own_row[h], HALF)
        ahead = lax.broadcasted_iota(jnp.int32, (HALF, 128), 1) - lax.broadcasted_iota(jnp.int32, (HALF, 128), 0)
        for k, lane in enumerate(lanes):
            paired = (ahead == text_row(p, c) + h * HALF - 128 * k).astype(F32)
            weights[block, lane] = (weigh(block, k) - paired).astype(BF16)

    def text_part(c_):
        lane = pl.ds(pl.multiple_of(c_ * (TEXTS // 2), TEXTS // 2), TEXTS // 2)
        return lax.dot_general(weights[:, lane], mol[...], (((0,), (0,)), ((), ())), preferred_element_type=F32)

    text_send[...] = text_part(1 - c).astype(BF16)
    send(text_send, text_recv0, 3, rs_sib_sem.at[0], sibling)
    text_sum[...] = text_part(c)

    def mol_parts(own):
        for h in (0, 1):
            block = rows(h * (MOLS // 2) + (q if own else other_q) * (MOLS // 4), MOLS // 4)
            part = jnp.dot(weights[block, :], text[...], preferred_element_type=F32)
            mol_sum[block, :] = part
            mol_send[block, :] = part.astype(BF16)
        q_ = q if own else other_q
        for e in (2, 1, 3, 0):
            starts = {}
            for d in (2, 1, 3):
                starts[0, d] = mol_row(0, q_, plus(x, e, 4), plus(y, d, 4))
                starts[1, d] = mol_row(1, q_, plus(x, d, 4), plus(y, e, 4))
            for d in (2, 1, 3):
                for h in (0, 1):
                    send(
                        mol_send.at[rows(starts[h, d], HALF)],
                        mol_recv1.at[h, own, e, d],
                        3,
                        rs_mol1_sem.at[own, e],
                        second_peer[h](d),
                    )

    mol_parts(0)

    await_rows(TEXTS // 2, rs_sib_sem.at[0])
    text_sum[...] = text_sum[...] + text_recv0[...].astype(F32)

    def text_block(d, part=(0, SHARD)):
        return text_sum[pl.ds(pl.multiple_of(plus(p, d, 8) * SHARD + part[0], HALF), part[1]), :]

    for slot, d in enumerate((4, 3, -3, 1, -1)):
        text_send1[slot] = text_block(d).astype(BF16)

    def text_pass(i, slot, part, d):
        span = pl.ds(part[0], part[1])
        send(text_send1.at[slot, span], text_recv1.at[slot, span], 3, rs_text_sem.at[i], p_peer(d))

    text_pass(1, 0, low, 2)
    text_pass(1, 0, high, -2)
    text_pass(0, 1, high, 1)
    text_pass(0, 2, low, -1)
    text_pass(1, 1, low, 1)
    text_pass(1, 2, high, -1)
    text_pass(2, 3, (0, SHARD), 1)
    text_pass(2, 4, (0, SHARD), -1)

    mol_parts(1)

    def text_pass2(d, part, *arrived):
        total = text_block(d, part)
        for slot in arrived:
            total = total + text_recv1[slot, pl.ds(*part), :].astype(F32)
        slot = 5 if d > 0 else 6
        text_send1[slot, pl.ds(*part), :] = total.astype(BF16)
        text_pass(2, slot, part, d)

    def mol_pass2(own, e):
        q_ = q if own else other_q
        await_rows(6 * HALF, rs_mol1_sem.at[own, e])
        for h in (0, 1):
            start = mol_row(0, q_, plus(x, e, 4), y) if h == 0 else mol_row(1, q_, x, plus(y, e, 4))
            block = mol_sum[rows(start, HALF), :]
            for d in (2, 1, 3):
                block = block + mol_recv1[h, own, e, d].astype(F32)
            if e == 0:
                mol_sum[rows(start, HALF), :] = block
            else:
                mol_send2[h, own, e] = block.astype(BF16)
                send(mol_send2.at[h, own, e], mol_recv2.at[h, own, e], 3, rs_mol2_sem.at[own], first_peer[h](e))

    def mol_total(own, h):
        block = mol_sum[rows(own_row[h] if own else partner_row[h], HALF), :]
        for d in (1, 3, 2):
            block = block + mol_recv2[h, own, d].astype(F32)
        return block

    mol_pass2(0, 2)
    await_rows(SHARD, rs_text_sem.at[0])
    text_pass2(2, high, 1)
    text_pass2(-2, low, 2)
    mol_pass2(0, 1)
    mol_pass2(0, 3)
    await_rows(2 * SHARD, rs_text_sem.at[1])
    text_pass2(2, low, 1, 0)
    text_pass2(-2, high, 2, 0)
    mol_pass2(0, 0)
    mol_pass2(1, 2)
    mol_pass2(1, 1)
    await_rows(6 * HALF, rs_mol2_sem.at[0])
    for h in (0, 1):
        mol_send3[h] = mol_total(0, h).astype(BF16)
        send(mol_send3.at[h], mol_recv3.at[h], 3, rs_pair_sem.at[0], partner)
    mol_pass2(1, 3)
    mol_pass2(1, 0)
    await_rows(4 * SHARD, rs_text_sem.at[2])
    total = text_block(0)
    for slot in (3, 4, 5, 6):
        total = total + text_recv1[slot].astype(F32)
    out[1] = total * INVERSE_TEMP
    await_rows(6 * HALF, rs_mol2_sem.at[1])
    await_rows(2 * HALF, rs_pair_sem.at[0])
    for h in (0, 1):
        out[0, pl.ds(HALF * h, HALF), :] = (mol_total(1, h) + mol_recv3[h].astype(F32)) * INVERSE_TEMP

    await_bytes(col_part.at[pl.ds(0, 15), pl.ds(0, 4)], sent_sem.at[1])
    await_bytes(row_part.at[pl.ds(0, 31)], sent_sem.at[2])
    await_rows(1472, sent_sem.at[3])


def on_device(molecules, texts):
    dma = pltpu.SemaphoreType.DMA
    both = pl.pallas_call(
        kernel,
        out_shape=jax.ShapeDtypeStruct((2, SHARD, D), F32),
        in_specs=[pl.BlockSpec(memory_space=pl.ANY)] * 2,
        out_specs=pl.BlockSpec(memory_space=pltpu.VMEM),
        scratch_shapes=[
            pltpu.VMEM((MOLS, D), BF16),
            pltpu.VMEM((TEXTS, D), BF16),
            pltpu.VMEM((MOLS, TEXTS), F32),
            pltpu.VMEM((MOLS, TEXTS), F32),
            pltpu.VMEM((MOLS, TEXTS), BF16),
            pltpu.VMEM((MOLS, 128), F32),
            pltpu.VMEM((8, 8, TEXTS), F32),
            pltpu.VMEM((8, 8, TEXTS), F32),
            pltpu.VMEM((32, 8, 128), F32),
            pltpu.VMEM((16, 8, 128), F32),
            pltpu.VMEM((MOLS, D), F32),
            pltpu.VMEM((MOLS, D), BF16),
            pltpu.VMEM((2, 2, 4, 4, HALF, D), BF16),
            pltpu.VMEM((2, 2, 4, HALF, D), BF16),
            pltpu.VMEM((2, 2, 4, HALF, D), BF16),
            pltpu.VMEM((2, HALF, D), BF16),
            pltpu.VMEM((2, HALF, D), BF16),
            pltpu.VMEM((TEXTS // 2, D), F32),
            pltpu.VMEM((TEXTS // 2, D), BF16),
            pltpu.VMEM((TEXTS // 2, D), BF16),
            pltpu.VMEM((7, SHARD, D), BF16),
            pltpu.VMEM((7, SHARD, D), BF16),
            dma((4,)),
            dma((1,)),
            dma((1,)),
            dma((2, 4)),
            dma((1,)),
            dma((5,)),
            dma((2,)),
            dma((1,)),
            dma((1,)),
            dma((1,)),
            dma((1,)),
            dma((3,)),
            dma((2, 4)),
            dma((2,)),
            dma((1,)),
        ],
        compiler_params=pltpu.CompilerParams(
            collective_id=0, has_side_effects=True, vmem_limit_bytes=60 << 20
        ),
    )(molecules, texts)
    return both[0], both[1]


def solution(mesh):
    spec = P(("blk", "grp"), None)
    return jax.shard_map(
        on_device, mesh=mesh, in_specs=(spec, spec), out_specs=(spec, spec), check_vma=False
    )
```

```python
import jax
import jax.numpy as jnp
from jax import lax
from jax.experimental import pallas as pl
from jax.experimental.pallas import tpu as pltpu
from jax.sharding import PartitionSpec as P

INVERSE_TEMP = 1.0 / 0.07
LOG2E = 1.4426950408889634
MESH = pl.DeviceIdType.MESH
F32 = jnp.float32
BF16 = jnp.bfloat16
D = 640
SHARD = 32
HALF = 16
MOLS = 1024
TEXTS = 512


def place():
    blk, grp = lax.axis_index("blk"), lax.axis_index("grp")
    x = lax.div(blk, 32)
    z = lax.rem(lax.div(blk, 2), 16)
    y = lax.rem(blk, 2) * 2 + lax.div(grp, 2)
    return x, y, lax.div(z, 2), lax.rem(z, 2), lax.rem(grp, 2)


def device(x, y, p, q, c):
    return ((x * 16 + p * 2 + q) * 2 + lax.div(y, 2), lax.rem(y, 2) * 2 + c)


def kernel(
    mol_in, text_in, out,
    mol, text, scores, by_row, weights, row_wide, col_top, col_mass, row_part, col_part,
    mol_sum, mol_send, mol_recv1, mol_send2, mol_recv2, mol_send3, mol_recv3,
    text_sum, text_send, text_recv0, text_send1, text_recv1,
    sent_sem, load_sem, pair_sem, mol1_sem, mol2_sem, near_sem, far_sem, sib_sem, row_sem, col_sem,
    rs_sib_sem, rs_text_sem, rs_mol1_sem, rs_mol2_sem, rs_pair_sem,
):
    x, y, p, q, c = place()

    def plus(v, d, n):
        return lax.rem(v + (d + n) % n, n)

    def x_peer(d):
        return device(plus(x, d, 4), y, p, q, c)

    def y_peer(d):
        return device(x, plus(y, d, 4), p, q, c)

    def p_peer(d):
        return device(x, y, plus(p, d, 8), q, c)

    partner = device(x, y, p, 1 - q, c)
    sibling = device(x, y, p, q, 1 - c)

    def send(src, dst, phase, sem, target):
        pltpu.make_async_remote_copy(
            src_ref=src,
            dst_ref=dst,
            send_sem=sent_sem.at[phase],
            recv_sem=sem,
            device_id=target,
            device_id_type=MESH,
        ).start()

    def await_bytes(ref, sem):
        pltpu.make_async_copy(ref, ref, sem).wait()

    def await_rows(count, sem):
        await_bytes(mol_sum.at[pl.ds(0, count // 2)], sem)

    def rows(start, size):
        return pl.ds(pl.multiple_of(start, 16), size)

    def mol_row(h, q_, x_, y_):
        return h * (MOLS // 2) + q_ * (MOLS // 4) + (y_ * 4 + x_ if h == 0 else x_ * 4 + y_) * HALF

    def text_row(p_, c_):
        return (c_ * 8 + p_) * SHARD

    other_q = 1 - q
    own_row = [mol_row(h, q, x, y) for h in (0, 1)]
    partner_row = [mol_row(h, other_q, x, y) for h in (0, 1)]
    loads = [
        pltpu.make_async_copy(mol_in.at[pl.ds(0, HALF)], mol.at[rows(own_row[0], HALF)], load_sem.at[0]),
        pltpu.make_async_copy(mol_in.at[pl.ds(HALF, HALF)], mol.at[rows(own_row[1], HALF)], load_sem.at[0]),
        pltpu.make_async_copy(text_in, text.at[rows(text_row(p, c), SHARD)], load_sem.at[0]),
    ]
    for load in loads:
        load.start()

    peers = [p_peer(d) for d in (1, -1, 2, -2)] + [partner, sibling]
    peers += [x_peer(d) for d in (1, 2, 3)] + [y_peer(d) for d in (1, 2, 3)]
    barrier = pltpu.get_barrier_semaphore()
    for peer in peers:
        pl.semaphore_signal(barrier, inc=1, device_id=peer, device_id_type=MESH)
    pl.semaphore_wait(barrier, len(peers))
    await_rows(2 * SHARD, load_sem.at[0])

    def text_send_rows(p_, c_, sem, target, first=0, size=SHARD):
        block = text.at[rows(text_row(p_, c_) + first, size)]
        send(block, block, 0, sem, target)

    def mol_send_rows(start, size, sem, target):
        block = mol.at[rows(start, size)]
        send(block, block, 0, sem, target)

    first_peer = [x_peer, y_peer]
    second_peer = [y_peer, x_peer]
    low, high = (0, HALF), (HALF, HALF)

    def fan(own):
        for d in (1, 3, 2):
            for h in (0, 1):
                start = own_row[h] if own else partner_row[h]
                mol_send_rows(start, HALF, mol1_sem.at[own, d], first_peer[h](d))

    def spread(own, e):
        q_ = q if own else other_q
        starts = [mol_row(0, q_, plus(x, e, 4), y), mol_row(1, q_, x, plus(y, e, 4))]
        for d in (1, 3, 2):
            for h in (0, 1):
                mol_send_rows(starts[h], HALF, mol2_sem.at[own], second_peer[h](d))

    def fan_arrived(own, e):
        await_rows(2 * HALF, mol1_sem.at[own, 4 - e])

    def to_sibling(d):
        text_send_rows(plus(p, d, 8), c, sib_sem.at[0], sibling)

    def forward(i, source, d, part):
        text_send_rows(plus(p, source, 8), c, far_sem.at[i], p_peer(d), *part)

    for i, (d, part) in enumerate(((2, low), (-2, high))):
        text_send_rows(p, c, near_sem.at[i], p_peer(d), *part)
    for h in (0, 1):
        mol_send_rows(own_row[h], HALF, pair_sem.at[0], partner)
    for i, (d, part) in enumerate(((2, high), (-2, low))):
        text_send_rows(p, c, near_sem.at[i + 2], p_peer(d), *part)
    fan(1)
    to_sibling(0)
    await_rows(2 * HALF, pair_sem.at[0])
    spread(0, 0)
    fan(0)
    fan_arrived(1, 2)
    spread(1, 2)
    await_rows(HALF, near_sem.at[0])
    forward(0, -2, 2, low)
    forward(1, -2, 1, low)
    fan_arrived(1, 1)
    spread(1, 1)
    fan_arrived(1, 3)
    spread(1, 3)
    await_rows(HALF, near_sem.at[1])
    forward(0, 2, -2, high)
    forward(1, 2, -1, high)
    for d in (1, -1):
        text_send_rows(p, c, near_sem.at[4], p_peer(d))
    await_rows(HALF, near_sem.at[2])
    forward(1, -2, 1, high)
    to_sibling(-2)
    await_rows(HALF, near_sem.at[3])
    forward(1, 2, -1, low)
    to_sibling(2)
    spread(1, 0)
    fan_arrived(0, 3)
    spread(0, 3)
    fan_arrived(0, 1)
    spread(0, 1)
    fan_arrived(0, 2)
    spread(0, 2)
    await_rows(2 * SHARD, near_sem.at[4])
    to_sibling(-1)
    to_sibling(1)
    await_rows(2 * SHARD, far_sem.at[1])
    to_sibling(-3)
    to_sibling(3)
    await_rows(SHARD, far_sem.at[0])
    to_sibling(4)
    await_rows(8 * SHARD, sib_sem.at[0])

    row_me = (x * 4 + y) * 2 + q
    col_me = c * 8 + p
    lanes = [slice(128 * k, 128 * k + 128) for k in range(TEXTS // 128)]

    def column_totals(b):
        for lane in lanes:
            tiles = scores[pl.ds(pl.multiple_of(b * 128, 128), 128), lane].reshape(16, 8, 128)
            top = jnp.max(tiles, axis=0)
            col_top[b, :, lane] = top
            col_mass[b, :, lane] = jnp.sum(jnp.exp2(tiles - top[None]), axis=0)

    def score(q_):
        for h in (0, 1):
            block = rows(mol_row(h, q_, 0, 0), MOLS // 4)
            scores[block, :] = lax.dot_general(
                mol[block, :], text[...], (((1,), (1,)), ((), ())), preferred_element_type=F32
            ) * (INVERSE_TEMP * LOG2E)
            for i in (0, 1):
                column_totals(h * 4 + q_ * 2 + i)

    await_rows(24 * HALF, mol2_sem.at[1])
    score(q)
    await_rows(24 * HALF, mol2_sem.at[0])
    score(other_q)
    await_rows(1472, sent_sem.at[0])
    for k, lane in enumerate(lanes):
        top = col_top[:, :, lane].reshape(64, 128)
        overall = jnp.max(top, axis=0, keepdims=True)
        mass = jnp.sum(col_mass[:, :, lane].reshape(64, 128) * jnp.exp2(top - overall), axis=0, keepdims=True)
        col_part[col_me, pl.ds(k, 1), :] = overall + jnp.log2(mass)
    for d in (4, 3, 5, 2, 6, 1, 7, 0):
        for e in (0, 1):
            if d or e:
                block = col_part.at[col_me, pl.ds(0, 4)]
                target = device(x, y, plus(p, d, 8), q, c if e == 0 else 1 - c)
                send(block, block, 1, col_sem.at[0], target)

    def row_totals(b, carry):
        block = pl.ds(pl.multiple_of(b * 128, 128), 128)
        parts = [scores[block, lane] for lane in lanes]
        top = jnp.maximum(jnp.maximum(parts[0], parts[1]), jnp.maximum(parts[2], parts[3]))
        mass = sum(jnp.exp2(part - top) for part in parts)
        top, mass = top.T, mass.T
        overall = jnp.max(top, axis=0, keepdims=True)
        mass = jnp.sum(mass * jnp.exp2(top - overall), axis=0, keepdims=True)
        row_part[row_me, pl.ds(b, 1), :] = overall + jnp.log2(mass)
        return carry

    lax.fori_loop(0, MOLS // 128, row_totals, 0)
    for dx in (2, 1, 3, 0):
        for dy in (2, 1, 3, 0):
            for e in (0, 1):
                if dx or dy or e:
                    block = row_part.at[row_me]
                    target = device(plus(x, dx, 4), plus(y, dy, 4), p, q if e == 0 else other_q, c)
                    send(block, block, 2, row_sem.at[0], target)

    def merge(parts):
        top = jnp.max(parts, axis=0)
        return top + jnp.log2(jnp.sum(jnp.exp2(parts - top[None]), axis=0))

    await_bytes(row_part.at[pl.ds(0, 31)], row_sem.at[0])
    row_lse = merge(row_part[...])
    for b in range(MOLS // 128):
        row_wide[128 * b : 128 * b + 128, :] = jnp.broadcast_to(row_lse[b : b + 1, :], (128, 128)).T

    def row_weight(b, carry):
        block = pl.ds(pl.multiple_of(b * 128, 128), 128)
        row = row_wide[block, :]
        for lane in lanes:
            by_row[block, lane] = 0.5 * jnp.exp2(scores[block, lane] - row)
        return carry

    lax.fori_loop(0, MOLS // 128, row_weight, 0)
    await_bytes(col_part.at[pl.ds(0, 15), pl.ds(0, 4)], col_sem.at[0])
    col_lse = merge(col_part[:, 0:4, :])

    def weigh(block, k):
        lane = lanes[k]
        return by_row[block, lane] + 0.5 * jnp.exp2(scores[block, lane] - col_lse[k : k + 1, :])

    def weight(b, carry):
        block = pl.ds(pl.multiple_of(b * 128, 128), 128)
        for k, lane in enumerate(lanes):
            weights[block, lane] = weigh(block, k).astype(BF16)
        return carry

    lax.fori_loop(0, MOLS // 128, weight, 0)
    for h in (0, 1):
        block = rows(own_row[h], HALF)
        ahead = lax.broadcasted_iota(jnp.int32, (HALF, 128), 1) - lax.broadcasted_iota(jnp.int32, (HALF, 128), 0)
        for k, lane in enumerate(lanes):
            paired = (ahead == text_row(p, c) + h * HALF - 128 * k).astype(F32)
            weights[block, lane] = (weigh(block, k) - paired).astype(BF16)

    def text_part(c_):
        lane = pl.ds(pl.multiple_of(c_ * (TEXTS // 2), TEXTS // 2), TEXTS // 2)
        return lax.dot_general(weights[:, lane], mol[...], (((0,), (0,)), ((), ())), preferred_element_type=F32)

    def mol_parts(own):
        for h in (0, 1):
            block = rows(h * (MOLS // 2) + (q if own else other_q) * (MOLS // 4), MOLS // 4)
            part = jnp.dot(weights[block, :], text[...], preferred_element_type=F32)
            mol_sum[block, :] = part
            mol_send[block, :] = part.astype(BF16)
        q_ = q if own else other_q
        for e in (2, 1, 3, 0):
            starts = {}
            for d in (2, 1, 3):
                starts[0, d] = mol_row(0, q_, plus(x, e, 4), plus(y, d, 4))
                starts[1, d] = mol_row(1, q_, plus(x, d, 4), plus(y, e, 4))
            for d in (2, 1, 3):
                for h in (0, 1):
                    send(
                        mol_send.at[rows(starts[h, d], HALF)],
                        mol_recv1.at[h, own, e, d],
                        3,
                        rs_mol1_sem.at[own, e],
                        second_peer[h](d),
                    )

    def text_block(d, part=(0, SHARD)):
        return text_sum[pl.ds(pl.multiple_of(plus(p, d, 8) * SHARD + part[0], HALF), part[1]), :]

    def text_pass(i, slot, part, d):
        span = pl.ds(part[0], part[1])
        send(text_send1.at[slot, span], text_recv1.at[slot, span], 3, rs_text_sem.at[i], p_peer(d))

    def text_pass2(d, part, *arrived):
        total = text_block(d, part)
        for slot in arrived:
            total = total + text_recv1[slot, pl.ds(*part), :].astype(F32)
        slot = 5 if d > 0 else 6
        text_send1[slot, pl.ds(*part), :] = total.astype(BF16)
        text_pass(2, slot, part, d)

    def mol_pass2(own, e):
        q_ = q if own else other_q
        await_rows(6 * HALF, rs_mol1_sem.at[own, e])
        for h in (0, 1):
            start = mol_row(0, q_, plus(x, e, 4), y) if h == 0 else mol_row(1, q_, x, plus(y, e, 4))
            block = mol_sum[rows(start, HALF), :]
            for d in (2, 1, 3):
                block = block + mol_recv1[h, own, e, d].astype(F32)
            if e == 0:
                mol_sum[rows(start, HALF), :] = block
            else:
                mol_send2[h, own, e] = block.astype(BF16)
                send(mol_send2.at[h, own, e], mol_recv2.at[h, own, e], 3, rs_mol2_sem.at[own], first_peer[h](e))

    def mol_total(own, h):
        block = mol_sum[rows(own_row[h] if own else partner_row[h], HALF), :]
        for d in (1, 3, 2):
            block = block + mol_recv2[h, own, d].astype(F32)
        return block

    text_send[...] = text_part(1 - c).astype(BF16)
    send(text_send, text_recv0, 3, rs_sib_sem.at[0], sibling)
    mol_parts(0)
    text_sum[...] = text_part(c)
    await_rows(TEXTS // 2, rs_sib_sem.at[0])
    text_sum[...] = text_sum[...] + text_recv0[...].astype(F32)
    for slot, d in enumerate((4, 3, -3, 1, -1)):
        text_send1[slot] = text_block(d).astype(BF16)

    text_pass(0, 1, high, 1)
    text_pass(0, 2, low, -1)
    text_pass(1, 0, low, 2)
    text_pass(1, 0, high, -2)
    text_pass(1, 1, low, 1)
    text_pass(1, 2, high, -1)
    mol_parts(1)
    mol_pass2(0, 2)
    await_rows(SHARD, rs_text_sem.at[0])
    text_pass2(2, high, 1)
    text_pass2(-2, low, 2)
    text_pass(2, 3, (0, SHARD), 1)
    text_pass(2, 4, (0, SHARD), -1)
    mol_pass2(0, 1)
    mol_pass2(0, 3)
    await_rows(2 * SHARD, rs_text_sem.at[1])
    text_pass2(2, low, 1, 0)
    text_pass2(-2, high, 2, 0)
    mol_pass2(0, 0)
    mol_pass2(1, 2)
    mol_pass2(1, 1)
    await_rows(6 * HALF, rs_mol2_sem.at[0])
    for h in (0, 1):
        mol_send3[h] = mol_total(0, h).astype(BF16)
        send(mol_send3.at[h], mol_recv3.at[h], 3, rs_pair_sem.at[0], partner)
    mol_pass2(1, 3)
    mol_pass2(1, 0)
    await_rows(4 * SHARD, rs_text_sem.at[2])
    total = text_block(0)
    for slot in (3, 4, 5, 6):
        total = total + text_recv1[slot].astype(F32)
    out[1] = total * INVERSE_TEMP
    await_rows(6 * HALF, rs_mol2_sem.at[1])
    await_rows(2 * HALF, rs_pair_sem.at[0])
    for h in (0, 1):
        out[0, pl.ds(HALF * h, HALF), :] = (mol_total(1, h) + mol_recv3[h].astype(F32)) * INVERSE_TEMP

    await_bytes(col_part.at[pl.ds(0, 15), pl.ds(0, 4)], sent_sem.at[1])
    await_bytes(row_part.at[pl.ds(0, 31)], sent_sem.at[2])
    await_rows(1472, sent_sem.at[3])


def on_device(molecules, texts):
    dma = pltpu.SemaphoreType.DMA
    both = pl.pallas_call(
        kernel,
        out_shape=jax.ShapeDtypeStruct((2, SHARD, D), F32),
        in_specs=[pl.BlockSpec(memory_space=pl.ANY)] * 2,
        out_specs=pl.BlockSpec(memory_space=pltpu.VMEM),
        scratch_shapes=[
            pltpu.VMEM((MOLS, D), BF16),
            pltpu.VMEM((TEXTS, D), BF16),
            pltpu.VMEM((MOLS, TEXTS), F32),
            pltpu.VMEM((MOLS, TEXTS), F32),
            pltpu.VMEM((MOLS, TEXTS), BF16),
            pltpu.VMEM((MOLS, 128), F32),
            pltpu.VMEM((8, 8, TEXTS), F32),
            pltpu.VMEM((8, 8, TEXTS), F32),
            pltpu.VMEM((32, 8, 128), F32),
            pltpu.VMEM((16, 8, 128), F32),
            pltpu.VMEM((MOLS, D), F32),
            pltpu.VMEM((MOLS, D), BF16),
            pltpu.VMEM((2, 2, 4, 4, HALF, D), BF16),
            pltpu.VMEM((2, 2, 4, HALF, D), BF16),
            pltpu.VMEM((2, 2, 4, HALF, D), BF16),
            pltpu.VMEM((2, HALF, D), BF16),
            pltpu.VMEM((2, HALF, D), BF16),
            pltpu.VMEM((TEXTS // 2, D), F32),
            pltpu.VMEM((TEXTS // 2, D), BF16),
            pltpu.VMEM((TEXTS // 2, D), BF16),
            pltpu.VMEM((7, SHARD, D), BF16),
            pltpu.VMEM((7, SHARD, D), BF16),
            dma((4,)),
            dma((1,)),
            dma((1,)),
            dma((2, 4)),
            dma((2,)),
            dma((5,)),
            dma((2,)),
            dma((1,)),
            dma((1,)),
            dma((1,)),
            dma((1,)),
            dma((3,)),
            dma((2, 4)),
            dma((2,)),
            dma((1,)),
        ],
        compiler_params=pltpu.CompilerParams(
            collective_id=0, has_side_effects=True, vmem_limit_bytes=60 << 20
        ),
    )(molecules, texts)
    return both[0], both[1]


def solution(mesh):
    spec = P(("blk", "grp"), None)
    return jax.shard_map(
        on_device, mesh=mesh, in_specs=(spec, spec), out_specs=(spec, spec), check_vma=False
    )
```

```python
import jax
import jax.numpy as jnp
from jax import lax
from jax.experimental import pallas as pl
from jax.experimental.pallas import tpu as pltpu
from jax.sharding import PartitionSpec as P

INVERSE_TEMP = 1.0 / 0.07
LOG2E = 1.4426950408889634
MESH = pl.DeviceIdType.MESH
F32 = jnp.float32
BF16 = jnp.bfloat16
D = 640
SHARD = 32
HALF = 16
MOLS = 1024
TEXTS = 512


def place():
    blk, grp = lax.axis_index("blk"), lax.axis_index("grp")
    x = lax.div(blk, 32)
    z = lax.rem(lax.div(blk, 2), 16)
    y = lax.rem(blk, 2) * 2 + lax.div(grp, 2)
    return x, y, lax.div(z, 2), lax.rem(z, 2), lax.rem(grp, 2)


def device(x, y, p, q, c):
    return ((x * 16 + p * 2 + q) * 2 + lax.div(y, 2), lax.rem(y, 2) * 2 + c)


def kernel(
    mol_in, text_in, out,
    mol, text, scores, by_row, weights, row_wide, col_top, col_mass, row_part, col_part,
    mol_sum, mol_send, mol_recv1, mol_send2, mol_recv2, mol_send3, mol_recv3,
    text_sum, text_send, text_recv0, text_send1, text_recv1,
    sent_sem, load_sem, pair_sem, mol1_sem, mol2_sem, near_sem, far_sem, sib_sem, row_sem, col_sem,
    rs_sib_sem, rs_text_sem, rs_mol1_sem, rs_mol2_sem, rs_pair_sem,
):
    x, y, p, q, c = place()

    def plus(v, d, n):
        return lax.rem(v + (d + n) % n, n)

    def x_peer(d):
        return device(plus(x, d, 4), y, p, q, c)

    def y_peer(d):
        return device(x, plus(y, d, 4), p, q, c)

    def p_peer(d):
        return device(x, y, plus(p, d, 8), q, c)

    partner = device(x, y, p, 1 - q, c)
    sibling = device(x, y, p, q, 1 - c)

    def send(src, dst, phase, sem, target):
        pltpu.make_async_remote_copy(
            src_ref=src,
            dst_ref=dst,
            send_sem=sent_sem.at[phase],
            recv_sem=sem,
            device_id=target,
            device_id_type=MESH,
        ).start()

    def await_bytes(ref, sem):
        pltpu.make_async_copy(ref, ref, sem).wait()

    def await_rows(count, sem):
        await_bytes(mol_sum.at[pl.ds(0, count // 2)], sem)

    def rows(start, size):
        return pl.ds(pl.multiple_of(start, 16), size)

    def mol_row(h, q_, x_, y_):
        return h * (MOLS // 2) + q_ * (MOLS // 4) + (y_ * 4 + x_ if h == 0 else x_ * 4 + y_) * HALF

    def text_row(p_, c_):
        return (c_ * 8 + p_) * SHARD

    other_q = 1 - q
    own_row = [mol_row(h, q, x, y) for h in (0, 1)]
    partner_row = [mol_row(h, other_q, x, y) for h in (0, 1)]
    loads = [
        pltpu.make_async_copy(mol_in.at[pl.ds(0, HALF)], mol.at[rows(own_row[0], HALF)], load_sem.at[0]),
        pltpu.make_async_copy(mol_in.at[pl.ds(HALF, HALF)], mol.at[rows(own_row[1], HALF)], load_sem.at[0]),
        pltpu.make_async_copy(text_in, text.at[rows(text_row(p, c), SHARD)], load_sem.at[0]),
    ]
    for load in loads:
        load.start()

    peers = [p_peer(d) for d in (1, -1, 2, -2)] + [partner, sibling]
    peers += [x_peer(d) for d in (1, 2, 3)] + [y_peer(d) for d in (1, 2, 3)]
    barrier = pltpu.get_barrier_semaphore()
    for peer in peers:
        pl.semaphore_signal(barrier, inc=1, device_id=peer, device_id_type=MESH)
    pl.semaphore_wait(barrier, len(peers))
    await_rows(2 * SHARD, load_sem.at[0])

    def text_send_rows(p_, c_, sem, target, first=0, size=SHARD):
        block = text.at[rows(text_row(p_, c_) + first, size)]
        send(block, block, 0, sem, target)

    def mol_send_rows(start, size, sem, target):
        block = mol.at[rows(start, size)]
        send(block, block, 0, sem, target)

    first_peer = [x_peer, y_peer]
    second_peer = [y_peer, x_peer]
    low, high = (0, HALF), (HALF, HALF)

    def fan(own):
        for d in (1, 3, 2):
            for h in (0, 1):
                start = own_row[h] if own else partner_row[h]
                mol_send_rows(start, HALF, mol1_sem.at[own, d], first_peer[h](d))

    def spread(own, e):
        q_ = q if own else other_q
        starts = [mol_row(0, q_, plus(x, e, 4), y), mol_row(1, q_, x, plus(y, e, 4))]
        for d in (1, 3, 2):
            for h in (0, 1):
                mol_send_rows(starts[h], HALF, mol2_sem.at[own], second_peer[h](d))

    def fan_arrived(own, e):
        await_rows(2 * HALF, mol1_sem.at[own, 4 - e])

    def to_sibling(d):
        text_send_rows(plus(p, d, 8), c, sib_sem.at[0], sibling)

    def forward(i, source, d, part):
        text_send_rows(plus(p, source, 8), c, far_sem.at[i], p_peer(d), *part)

    for i, (d, part) in enumerate(((2, low), (-2, high))):
        text_send_rows(p, c, near_sem.at[i], p_peer(d), *part)
    for h in (0, 1):
        mol_send_rows(own_row[h], HALF, pair_sem.at[0], partner)
    for i, (d, part) in enumerate(((2, high), (-2, low))):
        text_send_rows(p, c, near_sem.at[i + 2], p_peer(d), *part)
    fan(1)
    to_sibling(0)
    await_rows(2 * HALF, pair_sem.at[0])
    fan(0)
    spread(0, 0)
    fan_arrived(1, 1)
    spread(1, 1)
    fan_arrived(1, 3)
    spread(1, 3)
    await_rows(HALF, near_sem.at[1])
    forward(0, 2, -2, high)
    forward(1, 2, -1, high)
    await_rows(HALF, near_sem.at[0])
    forward(0, -2, 2, low)
    forward(1, -2, 1, low)
    fan_arrived(1, 2)
    spread(1, 2)
    for d in (1, -1):
        text_send_rows(p, c, near_sem.at[4], p_peer(d))
    await_rows(HALF, near_sem.at[2])
    forward(1, -2, 1, high)
    to_sibling(-2)
    await_rows(HALF, near_sem.at[3])
    forward(1, 2, -1, low)
    to_sibling(2)
    spread(1, 0)
    fan_arrived(0, 1)
    spread(0, 1)
    fan_arrived(0, 3)
    spread(0, 3)
    fan_arrived(0, 2)
    spread(0, 2)
    await_rows(2 * SHARD, near_sem.at[4])
    to_sibling(-1)
    to_sibling(1)
    await_rows(2 * SHARD, far_sem.at[1])
    to_sibling(-3)
    to_sibling(3)
    await_rows(SHARD, far_sem.at[0])
    to_sibling(4)
    await_rows(8 * SHARD, sib_sem.at[0])

    row_me = (x * 4 + y) * 2 + q
    col_me = c * 8 + p
    lanes = [slice(128 * k, 128 * k + 128) for k in range(TEXTS // 128)]

    def column_totals(b):
        for lane in lanes:
            tiles = scores[pl.ds(pl.multiple_of(b * 128, 128), 128), lane].reshape(16, 8, 128)
            top = jnp.max(tiles, axis=0)
            col_top[b, :, lane] = top
            col_mass[b, :, lane] = jnp.sum(jnp.exp2(tiles - top[None]), axis=0)

    def score(q_):
        for h in (0, 1):
            block = rows(mol_row(h, q_, 0, 0), MOLS // 4)
            scores[block, :] = lax.dot_general(
                mol[block, :], text[...], (((1,), (1,)), ((), ())), preferred_element_type=F32
            ) * (INVERSE_TEMP * LOG2E)
            for i in (0, 1):
                column_totals(h * 4 + q_ * 2 + i)

    await_rows(24 * HALF, mol2_sem.at[1])
    score(q)
    await_rows(24 * HALF, mol2_sem.at[0])
    score(other_q)
    await_rows(1472, sent_sem.at[0])
    for k, lane in enumerate(lanes):
        top = col_top[:, :, lane].reshape(64, 128)
        overall = jnp.max(top, axis=0, keepdims=True)
        mass = jnp.sum(col_mass[:, :, lane].reshape(64, 128) * jnp.exp2(top - overall), axis=0, keepdims=True)
        col_part[col_me, pl.ds(k, 1), :] = overall + jnp.log2(mass)
    for d in (4, 3, 5, 2, 6, 1, 7, 0):
        for e in (0, 1):
            if d or e:
                block = col_part.at[col_me, pl.ds(0, 4)]
                target = device(x, y, plus(p, d, 8), q, c if e == 0 else 1 - c)
                send(block, block, 1, col_sem.at[0], target)

    def row_totals(b, carry):
        block = pl.ds(pl.multiple_of(b * 128, 128), 128)
        parts = [scores[block, lane] for lane in lanes]
        top = jnp.maximum(jnp.maximum(parts[0], parts[1]), jnp.maximum(parts[2], parts[3]))
        mass = sum(jnp.exp2(part - top) for part in parts)
        top, mass = top.T, mass.T
        overall = jnp.max(top, axis=0, keepdims=True)
        mass = jnp.sum(mass * jnp.exp2(top - overall), axis=0, keepdims=True)
        row_part[row_me, pl.ds(b, 1), :] = overall + jnp.log2(mass)
        return carry

    lax.fori_loop(0, MOLS // 128, row_totals, 0)
    for x_ in range(4):
        for y_ in range(4):
            for e in (1, 0):
                def send_row():
                    block = row_part.at[row_me]
                    target = device(x_, y_, p, q if e == 0 else other_q, c)
                    send(block, block, 2, row_sem.at[0], target)

                if e:
                    send_row()
                else:
                    pl.when(jnp.logical_or(x != x_, y != y_))(send_row)

    def merge(parts):
        top = jnp.max(parts, axis=0)
        return top + jnp.log2(jnp.sum(jnp.exp2(parts - top[None]), axis=0))

    await_bytes(row_part.at[pl.ds(0, 31)], row_sem.at[0])
    row_lse = merge(row_part[...])
    for b in range(MOLS // 128):
        row_wide[128 * b : 128 * b + 128, :] = jnp.broadcast_to(row_lse[b : b + 1, :], (128, 128)).T

    def row_weight(b, carry):
        block = pl.ds(pl.multiple_of(b * 128, 128), 128)
        row = row_wide[block, :]
        for lane in lanes:
            by_row[block, lane] = 0.5 * jnp.exp2(scores[block, lane] - row)
        return carry

    lax.fori_loop(0, MOLS // 128, row_weight, 0)
    await_bytes(col_part.at[pl.ds(0, 15), pl.ds(0, 4)], col_sem.at[0])
    col_lse = merge(col_part[:, 0:4, :])

    def weigh(block, k):
        lane = lanes[k]
        return by_row[block, lane] + 0.5 * jnp.exp2(scores[block, lane] - col_lse[k : k + 1, :])

    def weight(b, carry):
        block = pl.ds(pl.multiple_of(b * 128, 128), 128)
        for k, lane in enumerate(lanes):
            weights[block, lane] = weigh(block, k).astype(BF16)
        return carry

    lax.fori_loop(0, MOLS // 128, weight, 0)
    for h in (0, 1):
        block = rows(own_row[h], HALF)
        ahead = lax.broadcasted_iota(jnp.int32, (HALF, 128), 1) - lax.broadcasted_iota(jnp.int32, (HALF, 128), 0)
        for k, lane in enumerate(lanes):
            paired = (ahead == text_row(p, c) + h * HALF - 128 * k).astype(F32)
            weights[block, lane] = (weigh(block, k) - paired).astype(BF16)

    def text_part(c_):
        lane = pl.ds(pl.multiple_of(c_ * (TEXTS // 2), TEXTS // 2), TEXTS // 2)
        return lax.dot_general(weights[:, lane], mol[...], (((0,), (0,)), ((), ())), preferred_element_type=F32)

    def mol_parts(own):
        for h in (0, 1):
            block = rows(h * (MOLS // 2) + (q if own else other_q) * (MOLS // 4), MOLS // 4)
            part = jnp.dot(weights[block, :], text[...], preferred_element_type=F32)
            mol_sum[block, :] = part
            mol_send[block, :] = part.astype(BF16)
        q_ = q if own else other_q
        for e in (2, 1, 3, 0):
            starts = {}
            for d in (2, 1, 3):
                starts[0, d] = mol_row(0, q_, plus(x, e, 4), plus(y, d, 4))
                starts[1, d] = mol_row(1, q_, plus(x, d, 4), plus(y, e, 4))
            for d in (2, 1, 3):
                for h in (0, 1):
                    send(
                        mol_send.at[rows(starts[h, d], HALF)],
                        mol_recv1.at[h, own, e, d],
                        3,
                        rs_mol1_sem.at[own, e],
                        second_peer[h](d),
                    )

    def text_block(d, part=(0, SHARD)):
        block = rows(plus(p, d, 8) * SHARD + part[0], part[1])
        return text_sum[block, :] + text_recv0[block, :].astype(F32)

    def text_pass(i, slot, part, d):
        span = pl.ds(part[0], part[1])
        send(text_send1.at[slot, span], text_recv1.at[slot, span], 3, rs_text_sem.at[i], p_peer(d))

    def text_pass2(d, part, *arrived):
        total = text_block(d, part)
        for slot in arrived:
            total = total + text_recv1[slot, pl.ds(*part), :].astype(F32)
        slot = 5 if d > 0 else 6
        text_send1[slot, pl.ds(*part), :] = total.astype(BF16)
        text_pass(2, slot, part, d)

    def mol_pass2(own, e):
        q_ = q if own else other_q
        await_rows(6 * HALF, rs_mol1_sem.at[own, e])
        for h in (0, 1):
            start = mol_row(0, q_, plus(x, e, 4), y) if h == 0 else mol_row(1, q_, x, plus(y, e, 4))
            block = mol_sum[rows(start, HALF), :]
            for d in (2, 1, 3):
                block = block + mol_recv1[h, own, e, d].astype(F32)
            if e == 0:
                mol_sum[rows(start, HALF), :] = block
            else:
                mol_send2[h, own, e] = block.astype(BF16)
                send(mol_send2.at[h, own, e], mol_recv2.at[h, own, e], 3, rs_mol2_sem.at[own], first_peer[h](e))

    def mol_total(own, h):
        block = mol_sum[rows(own_row[h] if own else partner_row[h], HALF), :]
        for d in (1, 3, 2):
            block = block + mol_recv2[h, own, d].astype(F32)
        return block

    text_send[...] = text_part(1 - c).astype(BF16)
    send(text_send, text_recv0, 3, rs_sib_sem.at[0], sibling)
    mol_parts(0)
    text_sum[...] = text_part(c)
    await_rows(TEXTS // 2, rs_sib_sem.at[0])
    def text_ready(slot, d):
        text_send1[slot] = text_block(d).astype(BF16)

    text_ready(1, 3)
    text_pass(0, 1, high, 1)
    text_ready(2, -3)
    text_pass(0, 2, low, -1)
    text_ready(0, 4)
    text_pass(1, 0, low, 2)
    text_pass(1, 0, high, -2)
    text_pass(1, 1, low, 1)
    text_pass(1, 2, high, -1)
    text_ready(3, 1)
    text_ready(4, -1)
    mol_parts(1)
    mol_pass2(0, 2)
    await_rows(SHARD, rs_text_sem.at[0])
    text_pass2(2, high, 1)
    text_pass2(-2, low, 2)
    text_pass(2, 3, (0, SHARD), 1)
    text_pass(2, 4, (0, SHARD), -1)
    mol_pass2(0, 1)
    mol_pass2(0, 3)
    await_rows(2 * SHARD, rs_text_sem.at[1])
    text_pass2(2, low, 1, 0)
    text_pass2(-2, high, 2, 0)
    mol_pass2(0, 0)
    mol_pass2(1, 2)
    mol_pass2(1, 1)
    await_rows(6 * HALF, rs_mol2_sem.at[0])
    for h in (0, 1):
        mol_send3[h] = mol_total(0, h).astype(BF16)
        send(mol_send3.at[h], mol_recv3.at[h], 3, rs_pair_sem.at[0], partner)
    mol_pass2(1, 3)
    mol_pass2(1, 0)
    await_rows(4 * SHARD, rs_text_sem.at[2])
    total = text_block(0)
    for slot in (3, 4, 5, 6):
        total = total + text_recv1[slot].astype(F32)
    out[1] = total * INVERSE_TEMP
    await_rows(6 * HALF, rs_mol2_sem.at[1])
    await_rows(2 * HALF, rs_pair_sem.at[0])
    for h in (0, 1):
        out[0, pl.ds(HALF * h, HALF), :] = (mol_total(1, h) + mol_recv3[h].astype(F32)) * INVERSE_TEMP

    await_bytes(col_part.at[pl.ds(0, 15), pl.ds(0, 4)], sent_sem.at[1])
    await_bytes(row_part.at[pl.ds(0, 31)], sent_sem.at[2])
    await_rows(1472, sent_sem.at[3])


def on_device(molecules, texts):
    dma = pltpu.SemaphoreType.DMA
    both = pl.pallas_call(
        kernel,
        out_shape=jax.ShapeDtypeStruct((2, SHARD, D), F32),
        in_specs=[pl.BlockSpec(memory_space=pl.ANY)] * 2,
        out_specs=pl.BlockSpec(memory_space=pltpu.VMEM),
        scratch_shapes=[
            pltpu.VMEM((MOLS, D), BF16),
            pltpu.VMEM((TEXTS, D), BF16),
            pltpu.VMEM((MOLS, TEXTS), F32),
            pltpu.VMEM((MOLS, TEXTS), F32),
            pltpu.VMEM((MOLS, TEXTS), BF16),
            pltpu.VMEM((MOLS, 128), F32),
            pltpu.VMEM((8, 8, TEXTS), F32),
            pltpu.VMEM((8, 8, TEXTS), F32),
            pltpu.VMEM((32, 8, 128), F32),
            pltpu.VMEM((16, 8, 128), F32),
            pltpu.VMEM((MOLS, D), F32),
            pltpu.VMEM((MOLS, D), BF16),
            pltpu.VMEM((2, 2, 4, 4, HALF, D), BF16),
            pltpu.VMEM((2, 2, 4, HALF, D), BF16),
            pltpu.VMEM((2, 2, 4, HALF, D), BF16),
            pltpu.VMEM((2, HALF, D), BF16),
            pltpu.VMEM((2, HALF, D), BF16),
            pltpu.VMEM((TEXTS // 2, D), F32),
            pltpu.VMEM((TEXTS // 2, D), BF16),
            pltpu.VMEM((TEXTS // 2, D), BF16),
            pltpu.VMEM((7, SHARD, D), BF16),
            pltpu.VMEM((7, SHARD, D), BF16),
            dma((4,)),
            dma((1,)),
            dma((1,)),
            dma((2, 4)),
            dma((2,)),
            dma((5,)),
            dma((2,)),
            dma((1,)),
            dma((1,)),
            dma((1,)),
            dma((1,)),
            dma((3,)),
            dma((2, 4)),
            dma((2,)),
            dma((1,)),
        ],
        compiler_params=pltpu.CompilerParams(
            collective_id=0, has_side_effects=True, vmem_limit_bytes=60 << 20
        ),
    )(molecules, texts)
    return both[0], both[1]


def solution(mesh):
    spec = P(("blk", "grp"), None)
    return jax.shard_map(
        on_device, mesh=mesh, in_specs=(spec, spec), out_specs=(spec, spec), check_vma=False
    )
```

```python
import jax
import jax.numpy as jnp
from jax import lax
from jax.experimental import pallas as pl
from jax.experimental.pallas import tpu as pltpu
from jax.sharding import PartitionSpec as P

INVERSE_TEMP = 1.0 / 0.07
LOG2E = 1.4426950408889634
MESH = pl.DeviceIdType.MESH
F32 = jnp.float32
BF16 = jnp.bfloat16
D = 640
SHARD = 32
HALF = 16
MOLS = 1024
TEXTS = 512


def place():
    blk, grp = lax.axis_index("blk"), lax.axis_index("grp")
    x = lax.div(blk, 32)
    z = lax.rem(lax.div(blk, 2), 16)
    y = lax.rem(blk, 2) * 2 + lax.div(grp, 2)
    return x, y, lax.div(z, 2), lax.rem(z, 2), lax.rem(grp, 2)


def device(x, y, p, q, c):
    return ((x * 16 + p * 2 + q) * 2 + lax.div(y, 2), lax.rem(y, 2) * 2 + c)


def kernel(
    mol_in, text_in, out,
    mol, text, scores, by_row, weights, row_wide, col_top, col_mass, row_part, col_part,
    mol_sum, mol_send, mol_recv1, mol_send2, mol_recv2, mol_send3, mol_recv3,
    text_sum, text_send, text_recv0, text_send1, text_recv1,
    sent_sem, load_sem, pair_sem, mol1_sem, mol2_sem, near_sem, far_sem, sib_sem, row_sem, col_sem,
    rs_sib_sem, rs_text_sem, rs_mol1_sem, rs_mol2_sem, rs_pair_sem,
):
    x, y, p, q, c = place()

    def plus(v, d, n):
        return lax.rem(v + (d + n) % n, n)

    def x_peer(d):
        return device(plus(x, d, 4), y, p, q, c)

    def y_peer(d):
        return device(x, plus(y, d, 4), p, q, c)

    def p_peer(d):
        return device(x, y, plus(p, d, 8), q, c)

    partner = device(x, y, p, 1 - q, c)
    sibling = device(x, y, p, q, 1 - c)

    def send(src, dst, phase, sem, target):
        pltpu.make_async_remote_copy(
            src_ref=src,
            dst_ref=dst,
            send_sem=sent_sem.at[phase],
            recv_sem=sem,
            device_id=target,
            device_id_type=MESH,
        ).start()

    def await_bytes(ref, sem):
        pltpu.make_async_copy(ref, ref, sem).wait()

    def await_rows(count, sem):
        await_bytes(mol_sum.at[pl.ds(0, count // 2)], sem)

    def rows(start, size):
        return pl.ds(pl.multiple_of(start, 16), size)

    def mol_row(h, q_, x_, y_):
        return h * (MOLS // 2) + q_ * (MOLS // 4) + (y_ * 4 + x_ if h == 0 else x_ * 4 + y_) * HALF

    def text_row(p_, c_):
        return (c_ * 8 + p_) * SHARD

    other_q = 1 - q
    own_row = [mol_row(h, q, x, y) for h in (0, 1)]
    partner_row = [mol_row(h, other_q, x, y) for h in (0, 1)]
    loads = [
        pltpu.make_async_copy(mol_in.at[pl.ds(0, HALF)], mol.at[rows(own_row[0], HALF)], load_sem.at[0]),
        pltpu.make_async_copy(mol_in.at[pl.ds(HALF, HALF)], mol.at[rows(own_row[1], HALF)], load_sem.at[0]),
        pltpu.make_async_copy(text_in, text.at[rows(text_row(p, c), SHARD)], load_sem.at[0]),
    ]
    for load in loads:
        load.start()

    peers = [p_peer(d) for d in (2, -2, 1, -1)] + [x_peer(d) for d in (2, 1, 3)]
    peers += [y_peer(d) for d in (2, 1, 3)] + [partner, sibling]
    barrier = pltpu.get_barrier_semaphore()
    for peer in peers:
        pl.semaphore_signal(barrier, inc=1, device_id=peer, device_id_type=MESH)
    pl.semaphore_wait(barrier, len(peers))
    await_rows(2 * SHARD, load_sem.at[0])

    def text_send_rows(p_, c_, sem, target, first=0, size=SHARD):
        block = text.at[rows(text_row(p_, c_) + first, size)]
        send(block, block, 0, sem, target)

    def mol_send_rows(start, size, sem, target):
        block = mol.at[rows(start, size)]
        send(block, block, 0, sem, target)

    first_peer = [x_peer, y_peer]
    second_peer = [y_peer, x_peer]
    low, high = (0, HALF), (HALF, HALF)

    def fan(own):
        for d in (1, 3, 2):
            for h in (0, 1):
                start = own_row[h] if own else partner_row[h]
                mol_send_rows(start, HALF, mol1_sem.at[own, d], first_peer[h](d))

    def spread(own, e):
        q_ = q if own else other_q
        starts = [mol_row(0, q_, plus(x, e, 4), y), mol_row(1, q_, x, plus(y, e, 4))]
        for d in (1, 3, 2):
            for h in (0, 1):
                mol_send_rows(starts[h], HALF, mol2_sem.at[own], second_peer[h](d))

    def fan_arrived(own, e):
        await_rows(2 * HALF, mol1_sem.at[own, 4 - e])

    def to_sibling(d):
        text_send_rows(plus(p, d, 8), c, sib_sem.at[0], sibling)

    def forward(i, source, d, part):
        text_send_rows(plus(p, source, 8), c, far_sem.at[i], p_peer(d), *part)

    for i, (d, part) in enumerate(((2, low), (-2, high))):
        text_send_rows(p, c, near_sem.at[i], p_peer(d), *part)
    for h in (0, 1):
        mol_send_rows(own_row[h], HALF, pair_sem.at[0], partner)
    for i, (d, part) in enumerate(((2, high), (-2, low))):
        text_send_rows(p, c, near_sem.at[i + 2], p_peer(d), *part)
    fan(1)
    to_sibling(0)
    await_rows(2 * HALF, pair_sem.at[0])
    fan(0)
    spread(0, 0)
    fan_arrived(1, 1)
    spread(1, 1)
    fan_arrived(1, 3)
    spread(1, 3)
    await_rows(HALF, near_sem.at[1])
    forward(0, 2, -2, high)
    forward(1, 2, -1, high)
    await_rows(HALF, near_sem.at[0])
    forward(0, -2, 2, low)
    forward(1, -2, 1, low)
    fan_arrived(1, 2)
    spread(1, 2)
    for d in (1, -1):
        text_send_rows(p, c, near_sem.at[4], p_peer(d))
    await_rows(HALF, near_sem.at[2])
    forward(1, -2, 1, high)
    to_sibling(-2)
    await_rows(HALF, near_sem.at[3])
    forward(1, 2, -1, low)
    to_sibling(2)
    spread(1, 0)
    fan_arrived(0, 1)
    spread(0, 1)
    fan_arrived(0, 3)
    spread(0, 3)
    fan_arrived(0, 2)
    spread(0, 2)
    await_rows(2 * SHARD, near_sem.at[4])
    to_sibling(-1)
    to_sibling(1)
    await_rows(2 * SHARD, far_sem.at[1])
    to_sibling(-3)
    to_sibling(3)
    await_rows(SHARD, far_sem.at[0])
    to_sibling(4)
    await_rows(8 * SHARD, sib_sem.at[0])

    row_me = (x * 4 + y) * 2 + q
    col_me = c * 8 + p
    lanes = [slice(128 * k, 128 * k + 128) for k in range(TEXTS // 128)]

    def column_totals(b):
        for lane in lanes:
            tiles = scores[pl.ds(pl.multiple_of(b * 128, 128), 128), lane].reshape(16, 8, 128)
            top = jnp.max(tiles, axis=0)
            col_top[b, :, lane] = top
            col_mass[b, :, lane] = jnp.sum(jnp.exp2(tiles - top[None]), axis=0)

    def score(q_):
        for h in (0, 1):
            block = rows(mol_row(h, q_, 0, 0), MOLS // 4)
            scores[block, :] = lax.dot_general(
                mol[block, :], text[...], (((1,), (1,)), ((), ())), preferred_element_type=F32
            ) * (INVERSE_TEMP * LOG2E)
            for i in (0, 1):
                column_totals(h * 4 + q_ * 2 + i)

    await_rows(24 * HALF, mol2_sem.at[1])
    score(q)
    await_rows(24 * HALF, mol2_sem.at[0])
    score(other_q)
    await_rows(1472, sent_sem.at[0])
    for k, lane in enumerate(lanes):
        top = col_top[:, :, lane].reshape(64, 128)
        overall = jnp.max(top, axis=0, keepdims=True)
        mass = jnp.sum(col_mass[:, :, lane].reshape(64, 128) * jnp.exp2(top - overall), axis=0, keepdims=True)
        col_part[col_me, pl.ds(k, 1), :] = overall + jnp.log2(mass)
    for d in (4, 3, 5, 2, 6, 1, 7, 0):
        for e in (0, 1):
            if d or e:
                block = col_part.at[col_me, pl.ds(0, 4)]
                target = device(x, y, plus(p, d, 8), q, c if e == 0 else 1 - c)
                send(block, block, 1, col_sem.at[0], target)

    def row_totals(b, carry):
        block = pl.ds(pl.multiple_of(b * 128, 128), 128)
        parts = [scores[block, lane] for lane in lanes]
        top = jnp.maximum(jnp.maximum(parts[0], parts[1]), jnp.maximum(parts[2], parts[3]))
        mass = sum(jnp.exp2(part - top) for part in parts)
        top, mass = top.T, mass.T
        overall = jnp.max(top, axis=0, keepdims=True)
        mass = jnp.sum(mass * jnp.exp2(top - overall), axis=0, keepdims=True)
        row_part[row_me, pl.ds(b, 1), :] = overall + jnp.log2(mass)
        return carry

    lax.fori_loop(0, MOLS // 128, row_totals, 0)
    for x_ in range(4):
        for y_ in range(4):
            for e in (1, 0):
                def send_row():
                    block = row_part.at[row_me]
                    target = device(x_, y_, p, q if e == 0 else other_q, c)
                    send(block, block, 2, row_sem.at[0], target)

                if e:
                    send_row()
                else:
                    pl.when(jnp.logical_or(x != x_, y != y_))(send_row)

    def merge(parts):
        top = jnp.max(parts, axis=0)
        return top + jnp.log2(jnp.sum(jnp.exp2(parts - top[None]), axis=0))

    await_bytes(row_part.at[pl.ds(0, 31)], row_sem.at[0])
    row_lse = merge(row_part[...])
    for b in range(MOLS // 128):
        row_wide[128 * b : 128 * b + 128, :] = jnp.broadcast_to(row_lse[b : b + 1, :], (128, 128)).T

    def row_weight(b, carry):
        block = pl.ds(pl.multiple_of(b * 128, 128), 128)
        row = row_wide[block, :]
        for lane in lanes:
            by_row[block, lane] = 0.5 * jnp.exp2(scores[block, lane] - row)
        return carry

    lax.fori_loop(0, MOLS // 128, row_weight, 0)
    await_bytes(col_part.at[pl.ds(0, 15), pl.ds(0, 4)], col_sem.at[0])
    col_lse = merge(col_part[:, 0:4, :])

    def weigh(block, k):
        lane = lanes[k]
        return by_row[block, lane] + 0.5 * jnp.exp2(scores[block, lane] - col_lse[k : k + 1, :])

    def weight(b, carry):
        block = pl.ds(pl.multiple_of(b * 128, 128), 128)
        for k, lane in enumerate(lanes):
            weights[block, lane] = weigh(block, k).astype(BF16)
        return carry

    lax.fori_loop(0, MOLS // 128, weight, 0)
    for h in (0, 1):
        block = rows(own_row[h], HALF)
        ahead = lax.broadcasted_iota(jnp.int32, (HALF, 128), 1) - lax.broadcasted_iota(jnp.int32, (HALF, 128), 0)
        for k, lane in enumerate(lanes):
            paired = (ahead == text_row(p, c) + h * HALF - 128 * k).astype(F32)
            weights[block, lane] = (weigh(block, k) - paired).astype(BF16)

    def text_part(c_):
        lane = pl.ds(pl.multiple_of(c_ * (TEXTS // 2), TEXTS // 2), TEXTS // 2)
        return lax.dot_general(weights[:, lane], mol[...], (((0,), (0,)), ((), ())), preferred_element_type=F32)

    def mol_parts(own):
        for h in (0, 1):
            block = rows(h * (MOLS // 2) + (q if own else other_q) * (MOLS // 4), MOLS // 4)
            part = jnp.dot(weights[block, :], text[...], preferred_element_type=F32)
            mol_sum[block, :] = part
            mol_send[block, :] = part.astype(BF16)
        q_ = q if own else other_q
        for e in (2, 1, 3, 0):
            starts = {}
            for d in (2, 1, 3):
                starts[0, d] = mol_row(0, q_, plus(x, e, 4), plus(y, d, 4))
                starts[1, d] = mol_row(1, q_, plus(x, d, 4), plus(y, e, 4))
            for d in (2, 1, 3):
                for h in (0, 1):
                    send(
                        mol_send.at[rows(starts[h, d], HALF)],
                        mol_recv1.at[h, own, e, d],
                        3,
                        rs_mol1_sem.at[own, e],
                        second_peer[h](d),
                    )

    def text_block(d, part=(0, SHARD)):
        block = rows(plus(p, d, 8) * SHARD + part[0], part[1])
        return text_sum[block, :] + text_recv0[block, :].astype(F32)

    def text_pass(i, slot, part, d):
        span = pl.ds(part[0], part[1])
        send(text_send1.at[slot, span], text_recv1.at[slot, span], 3, rs_text_sem.at[i], p_peer(d))

    def text_pass2(d, part, *arrived):
        total = text_block(d, part)
        for slot in arrived:
            total = total + text_recv1[slot, pl.ds(*part), :].astype(F32)
        slot = 5 if d > 0 else 6
        text_send1[slot, pl.ds(*part), :] = total.astype(BF16)
        text_pass(2, slot, part, d)

    def mol_pass2(own, e):
        q_ = q if own else other_q
        await_rows(6 * HALF, rs_mol1_sem.at[own, e])
        for h in (0, 1):
            start = mol_row(0, q_, plus(x, e, 4), y) if h == 0 else mol_row(1, q_, x, plus(y, e, 4))
            block = mol_sum[rows(start, HALF), :]
            for d in (2, 1, 3):
                block = block + mol_recv1[h, own, e, d].astype(F32)
            if e == 0:
                mol_sum[rows(start, HALF), :] = block
            else:
                mol_send2[h, own, e] = block.astype(BF16)
                send(mol_send2.at[h, own, e], mol_recv2.at[h, own, e], 3, rs_mol2_sem.at[own], first_peer[h](e))

    def mol_total(own, h):
        block = mol_sum[rows(own_row[h] if own else partner_row[h], HALF), :]
        for d in (1, 3, 2):
            block = block + mol_recv2[h, own, d].astype(F32)
        return block

    text_send[...] = text_part(1 - c).astype(BF16)
    send(text_send, text_recv0, 3, rs_sib_sem.at[0], sibling)
    mol_parts(0)
    text_sum[...] = text_part(c)
    await_rows(TEXTS // 2, rs_sib_sem.at[0])
    def text_ready(slot, d):
        text_send1[slot] = text_block(d).astype(BF16)

    text_ready(1, 3)
    text_pass(0, 1, high, 1)
    text_ready(2, -3)
    text_pass(0, 2, low, -1)
    text_ready(0, 4)
    text_pass(1, 0, low, 2)
    text_pass(1, 0, high, -2)
    text_pass(1, 1, low, 1)
    text_pass(1, 2, high, -1)
    text_ready(3, 1)
    text_ready(4, -1)
    mol_parts(1)
    mol_pass2(0, 2)
    await_rows(SHARD, rs_text_sem.at[0])
    text_pass2(2, high, 1)
    text_pass2(-2, low, 2)
    text_pass(2, 3, (0, SHARD), 1)
    text_pass(2, 4, (0, SHARD), -1)
    mol_pass2(0, 1)
    mol_pass2(0, 3)
    await_rows(2 * SHARD, rs_text_sem.at[1])
    text_pass2(2, low, 1, 0)
    text_pass2(-2, high, 2, 0)
    mol_pass2(0, 0)
    mol_pass2(1, 2)
    mol_pass2(1, 1)
    await_rows(6 * HALF, rs_mol2_sem.at[0])
    for h in (0, 1):
        mol_send3[h] = mol_total(0, h).astype(BF16)
        send(mol_send3.at[h], mol_recv3.at[h], 3, rs_pair_sem.at[0], partner)
    mol_pass2(1, 3)
    mol_pass2(1, 0)
    await_rows(4 * SHARD, rs_text_sem.at[2])
    total = text_block(0)
    for slot in (3, 4, 5, 6):
        total = total + text_recv1[slot].astype(F32)
    out[1] = total * INVERSE_TEMP
    await_rows(6 * HALF, rs_mol2_sem.at[1])
    await_rows(2 * HALF, rs_pair_sem.at[0])
    for h in (0, 1):
        out[0, pl.ds(HALF * h, HALF), :] = (mol_total(1, h) + mol_recv3[h].astype(F32)) * INVERSE_TEMP

    await_bytes(col_part.at[pl.ds(0, 15), pl.ds(0, 4)], sent_sem.at[1])
    await_bytes(row_part.at[pl.ds(0, 31)], sent_sem.at[2])
    await_rows(1472, sent_sem.at[3])


def on_device(molecules, texts):
    dma = pltpu.SemaphoreType.DMA
    both = pl.pallas_call(
        kernel,
        out_shape=jax.ShapeDtypeStruct((2, SHARD, D), F32),
        in_specs=[pl.BlockSpec(memory_space=pl.ANY)] * 2,
        out_specs=pl.BlockSpec(memory_space=pltpu.VMEM),
        scratch_shapes=[
            pltpu.VMEM((MOLS, D), BF16),
            pltpu.VMEM((TEXTS, D), BF16),
            pltpu.VMEM((MOLS, TEXTS), F32),
            pltpu.VMEM((MOLS, TEXTS), F32),
            pltpu.VMEM((MOLS, TEXTS), BF16),
            pltpu.VMEM((MOLS, 128), F32),
            pltpu.VMEM((8, 8, TEXTS), F32),
            pltpu.VMEM((8, 8, TEXTS), F32),
            pltpu.VMEM((32, 8, 128), F32),
            pltpu.VMEM((16, 8, 128), F32),
            pltpu.VMEM((MOLS, D), F32),
            pltpu.VMEM((MOLS, D), BF16),
            pltpu.VMEM((2, 2, 4, 4, HALF, D), BF16),
            pltpu.VMEM((2, 2, 4, HALF, D), BF16),
            pltpu.VMEM((2, 2, 4, HALF, D), BF16),
            pltpu.VMEM((2, HALF, D), BF16),
            pltpu.VMEM((2, HALF, D), BF16),
            pltpu.VMEM((TEXTS // 2, D), F32),
            pltpu.VMEM((TEXTS // 2, D), BF16),
            pltpu.VMEM((TEXTS // 2, D), BF16),
            pltpu.VMEM((7, SHARD, D), BF16),
            pltpu.VMEM((7, SHARD, D), BF16),
            dma((4,)),
            dma((1,)),
            dma((1,)),
            dma((2, 4)),
            dma((2,)),
            dma((5,)),
            dma((2,)),
            dma((1,)),
            dma((1,)),
            dma((1,)),
            dma((1,)),
            dma((3,)),
            dma((2, 4)),
            dma((2,)),
            dma((1,)),
        ],
        compiler_params=pltpu.CompilerParams(
            collective_id=0, has_side_effects=True, vmem_limit_bytes=60 << 20
        ),
    )(molecules, texts)
    return both[0], both[1]


def solution(mesh):
    spec = P(("blk", "grp"), None)
    return jax.shard_map(
        on_device, mesh=mesh, in_specs=(spec, spec), out_specs=(spec, spec), check_vma=False
    )
```
